128 devices in a mesh: dom: 32 (over x, y, core), rep: 4 (over z).
Axes of the slice: x: 4, y: 4, z: 4, core: 2. Of those that a mesh axis runs over, the one named last changes fastest.
Arguments:
- features: float32 [256, 65536], P('rep', 'dom'), may hold values from -6 to 6
- weight: float32 [256, 256], replicated, may hold values from -0.375 to 0.375
- bias: float32 [256], P('rep'), may hold values from -3 to 3
- cotangent: float32 [256, 65536], P('rep', 'dom'), may hold values from -6 to 6
- send_index: int32 [32, 4096], P('dom'), may hold values from 0 to 2047
- send_count: int32 [32, 32], P('dom'), may hold values from 0 to 128, as said below
- hub_local: int32 [4096], P('dom'), may hold values from 0 to 2047, as said below
- low_tiles: float32 [4096, 128, 128], P('dom'), may hold values from -0.15625 to 0.15625
- low_src: int32 [4096], P('dom'), may hold values from 0 to 31
- low_dst: int32 [4096], P('dom'), may hold values from 0 to 15
- hub_tiles: float32 [2048, 128, 128], P('dom'), may hold values from -0.15625 to 0.15625
- hub_src: int32 [2048], P('dom'), may hold values from 0 to 31
- hub_dst: int32 [2048], P('dom'), may hold values from 0 to 15
Outputs:
- output: float32 [256, 65536], P('rep', 'dom')
- feature_grad: float32 [256, 65536], P('rep', 'dom')
- weight_grad: float32 [256, 256], P('rep')
- bias_grad: float32 [256], P('rep')
The draws below stay inside these ranges and needn't reach their ends.
Inputs may be any that keep to these rules, and one draw needn't show every extreme that they name: `send_count`: live slots are counted from the start of each block of 128; in every draw some device receives 128 live rows from every device. `hub_local`: distinct within each owning device.
All inputs are finite; a program needn't handle non-finite values.
Results may differ from the reference program's by a relative error of at most 0.0003.
Values sent between devices are 32-bit elements; how exact they have to be, the bound alone decides.
A program may use at most 128 MiB of HBM per device.

```python
import math
import jax
import jax.numpy as jnp
from jax import lax

F = 256
VDEV = 2048
C = 128
NHUB = 4096
TB = 128
LT = 128
HT = 64
V = 65536
HUB_DEV = 128
NB = 16
RB = 32
HB = 32
N_DOM = 32


def draw_send_count(key, part):
    key = jax.random.fold_in(key, 11)
    first_key, second_key = jax.random.split(key)
    counts = jax.random.randint(first_key, (N_DOM, N_DOM), 0, C + 1)
    target = jax.random.randint(second_key, (), 0, N_DOM)
    column = jnp.arange(N_DOM)[None, :]
    return jnp.where(column == target, C, counts).astype(jnp.int32)


def pick_hubs(subkey):
    return jax.random.permutation(subkey, VDEV)[:HUB_DEV]


def draw_hub_local(key, part):
    key = jax.random.fold_in(key, 23)
    subkeys = jax.random.split(key, N_DOM)
    return jax.vmap(pick_hubs)(subkeys).reshape(NHUB).astype(jnp.int32)


def set_ends(entries, key, least, largest):
    longest = entries.shape.index(max(entries.shape))
    spots = []
    for shift in (0, 1):
        where = [jax.random.randint(jax.random.fold_in(key, axis), (), 0, length) for axis, length in enumerate(entries.shape)]
        where[longest] = (where[longest] + shift) % entries.shape[longest]
        spots.append(tuple(where))
    return entries.at[spots[0]].set(least).at[spots[1]].set(largest)


def shard_levels(key, extent, cuts, low, high):
    factor_of, own = 1.0, jax.random.fold_in(key, 6)
    for dim, shards_of in cuts:
        draws = jnp.exp(jax.random.uniform(jax.random.fold_in(own, dim), (shards_of,), jnp.float32, low / len(cuts), high / len(cuts)))
        factor_of = factor_of * jnp.repeat(draws, extent[dim] // shards_of).reshape([-1 if axis == dim else 1 for axis in range(len(extent))])
    return factor_of


def centred(own_key, extent, deviation, bound, cuts=(), kind=jnp.bfloat16):
    entries = jax.random.normal(own_key, extent, jnp.float32) * deviation
    if len(cuts) > 0:
        entries = shard_levels(own_key, extent, cuts, -0.22, 0.18) * entries
    return jnp.clip(entries, min=-bound, max=bound).astype(kind)


def setup_inputs(seed: int = 0) -> dict:
    key_list = jax.random.split(jax.random.key(seed), 14)
    features = centred(key_list[0], (F, V), 1.0, 6.0, ((0, 4), (1, 32)), jnp.float32)
    weight = centred(key_list[1], (F, F), F ** -0.5, 0.375, (), jnp.float32)
    bias = centred(key_list[2], (F,), 0.5, 3.0, ((0, 4),), jnp.float32)
    cotangent = centred(key_list[3], (F, V), 1.0, 6.0, ((0, 4), (1, 32)), jnp.float32)
    send_index = set_ends(jax.random.randint(key_list[4], (N_DOM, N_DOM * C), 0, VDEV), jax.random.fold_in(key_list[4], 1), 0, VDEV - 1).astype(jnp.int32)
    send_count = draw_send_count(jax.random.fold_in(key_list[13], 71), 0)
    hub_local = draw_hub_local(jax.random.fold_in(key_list[13], 71), 0)
    low_tiles = centred(key_list[7], (N_DOM * LT, TB, TB), (TB * (LT + HT) // NB) ** -0.5, 0.15625, ((0, 32),), jnp.float32)
    low_src = set_ends(jax.random.randint(key_list[8], (N_DOM * LT,), 0, RB), jax.random.fold_in(key_list[8], 1), 0, RB - 1).astype(jnp.int32)
    low_dst = set_ends(jax.random.randint(key_list[9], (N_DOM * LT,), 0, NB), jax.random.fold_in(key_list[9], 1), 0, NB - 1).astype(jnp.int32)
    hub_tiles = centred(key_list[10], (N_DOM * HT, TB, TB), (TB * (LT + HT) // NB) ** -0.5, 0.15625, ((0, 32),), jnp.float32)
    hub_src = set_ends(jax.random.randint(key_list[11], (N_DOM * HT,), 0, HB), jax.random.fold_in(key_list[11], 1), 0, HB - 1).astype(jnp.int32)
    hub_dst = set_ends(jax.random.randint(key_list[12], (N_DOM * HT,), 0, NB), jax.random.fold_in(key_list[12], 1), 0, NB - 1).astype(jnp.int32)
    return {"features": features, "weight": weight, "bias": bias, "cotangent": cotangent, "send_index": send_index, "send_count": send_count, "hub_local": hub_local, "low_tiles": low_tiles, "low_src": low_src, "low_dst": low_dst, "hub_tiles": hub_tiles, "hub_src": hub_src, "hub_dst": hub_dst}


HIGH = lax.Precision.HIGHEST

def forward_tiles(source, tile_vals, src_ids, dst_ids, dst_blocks):
    width = source.shape[0]
    edge = tile_vals.shape[1]
    source_blocks = source.reshape(width, -1, edge)
    picked = jnp.take(source_blocks, src_ids, axis=1)
    product = jnp.einsum('ftq,tpq->ftp', picked, tile_vals, precision=HIGH)
    onehot = (dst_ids[:, None] == jnp.arange(dst_blocks, dtype=jnp.int32)[None, :]).astype(jnp.float32)
    result = jnp.einsum('ftp,tb->fbp', product, onehot, precision=HIGH)
    return result.reshape(width, dst_blocks * edge)

def backward_tiles(grad, tile_vals, src_ids, dst_ids, src_blocks):
    width = grad.shape[0]
    edge = tile_vals.shape[1]
    grad_blocks = grad.reshape(width, -1, edge)
    picked = jnp.take(grad_blocks, dst_ids, axis=1)
    product = jnp.einsum('ftp,tpq->ftq', picked, tile_vals, precision=HIGH)
    onehot = (src_ids[:, None] == jnp.arange(src_blocks, dtype=jnp.int32)[None, :]).astype(jnp.float32)
    result = jnp.einsum('ftq,ts->fsq', product, onehot, precision=HIGH)
    return result.reshape(width, src_blocks * edge)

def take_columns(local_rows, indices):
    return jnp.take(local_rows, indices, axis=1)

def add_columns(values, indices):
    return jnp.zeros((F, VDEV), jnp.float32).at[:, indices].add(values)

def reference(features, weight, bias, cotangent, send_index, send_count, hub_local, low_tiles, low_src, low_dst, hub_tiles, hub_src, hub_dst):
    slots = jnp.arange(N_DOM * C, dtype=jnp.int32)
    live = ((slots % C)[None, :] < jnp.repeat(send_count, C, axis=1)).astype(jnp.float32)
    per_device = features.reshape(F, N_DOM, VDEV).transpose(1, 0, 2)
    outgoing = jax.vmap(take_columns)(per_device, send_index) * live[:, None, :]
    received = outgoing.reshape(N_DOM, F, N_DOM, C).transpose(2, 1, 0, 3).reshape(N_DOM, F, N_DOM * C)
    hub_global = (jnp.arange(NHUB, dtype=jnp.int32) // HUB_DEV * VDEV + hub_local).astype(jnp.int32)
    hub_rows = jnp.take(features, hub_global, axis=1)
    low_four = low_tiles.reshape(N_DOM, LT, TB, TB)
    hub_four = hub_tiles.reshape(N_DOM, HT, TB, TB)
    low_src2 = low_src.reshape(N_DOM, LT)
    low_dst2 = low_dst.reshape(N_DOM, LT)
    hub_src2 = hub_src.reshape(N_DOM, HT)
    hub_dst2 = hub_dst.reshape(N_DOM, HT)

    def aggregate_one(items):
        rows_in, ltile, lsrc, ldst, htile, hsrc, hdst = items
        low_part = forward_tiles(rows_in, ltile, lsrc, ldst, NB)
        return low_part + forward_tiles(hub_rows, htile, hsrc, hdst, NB)
    summed3 = lax.map(aggregate_one, (received, low_four, low_src2, low_dst2, hub_four, hub_src2, hub_dst2))
    summed = summed3.transpose(1, 0, 2).reshape(F, V)
    pre = lax.dot_general(weight, summed, (((0,), (0,)), ((), ())), precision=HIGH) + bias[:, None]
    sig = jax.nn.sigmoid(pre)
    output = pre * sig
    pre_grad = cotangent * sig * (1.0 + pre * (1.0 - sig))
    summed_grad = jnp.dot(weight, pre_grad, precision=HIGH)
    scale = 1.0 / math.sqrt(V)
    weight_grad = lax.dot_general(summed, pre_grad, (((1,), (1,)), ((), ())), precision=HIGH) * scale
    bias_grad = lax.optimization_barrier(jnp.sum(pre_grad, axis=1)) * scale
    grad3 = summed_grad.reshape(F, N_DOM, VDEV).transpose(1, 0, 2)

    def back_one(items):
        grad_in, ltile, lsrc, ldst, htile, hsrc, hdst = items
        return (backward_tiles(grad_in, ltile, lsrc, ldst, RB), backward_tiles(grad_in, htile, hsrc, hdst, HB))
    low_back, hub_back = lax.map(back_one, (grad3, low_four, low_src2, low_dst2, hub_four, hub_src2, hub_dst2))
    hub_grad = lax.optimization_barrier(jnp.sum(hub_back, axis=0))
    returned = low_back.reshape(N_DOM, F, N_DOM, C).transpose(2, 1, 0, 3).reshape(N_DOM, F, N_DOM * C) * live[:, None, :]
    grads3 = jax.vmap(add_columns)(returned, send_index)
    feature_grad = grads3.transpose(1, 0, 2).reshape(F, V).at[:, hub_global].add(hub_grad)
    return (output, feature_grad, weight_grad, bias_grad)
```

```python
import math

import jax
import jax.numpy as jnp
from jax import lax
from jax.experimental import pallas as pl
from jax.experimental.pallas import tpu as pltpu
from jax.sharding import PartitionSpec as P

F32 = jnp.float32
BF16 = jnp.bfloat16
I32 = jnp.int32
NN = (((1,), (0,)), ((), ()))
NT = (((1,), (1,)), ((), ()))
MESH = pl.DeviceIdType.MESH

FL = 64
VD = 2048
CH = 512
B = 128
LT, HT = 128, 64
NB = 16
UNROLL = 16

LOW, BACK = 0, 32
COT, BIAS, SUM, GRAD, OUT, WZ = 64, 67, 70, 73, 76, 79
HUB1A, HUB1B, HUB2A, HUB2B, HUB3 = 82, 85, 88, 91, 94
RED0, RED1A, RED1B, RED2A, RED2B = 96, 97, 100, 103, 106
WC, WX, WY, WC2 = 109, 110, 113, 116
NSEM = 117


def mm(a, b, dims):
    return lax.dot_general(a, b, dims, preferred_element_type=F32)


def split(x):
    high = x.astype(BF16)
    return high, (x - high.astype(F32)).astype(BF16)


def fold(r):
    return r[:FL] + r[FL:]


def place(idx):
    return (lax.broadcasted_iota(I32, (VD, idx.shape[1]), 0) == idx).astype(BF16)


def order(key, other):
    n = key.shape[1]
    lane = lax.broadcasted_iota(I32, (n, n), 1)
    sub = lax.broadcasted_iota(I32, (n, n), 0)
    eye = lane == sub
    key = jnp.broadcast_to(key, (n, n))
    other = jnp.broadcast_to(other, (n, n))
    key_col = jnp.sum(jnp.where(eye, key, 0), axis=1, keepdims=True)
    other_col = jnp.sum(jnp.where(eye, other, 0), axis=1, keepdims=True)
    less = jnp.sum(jnp.where(key < key_col, 1, 0), axis=1, keepdims=True)
    before = (key == key_col) & (lane < sub)
    rank = less + jnp.sum(jnp.where(before, 1, 0), axis=1, keepdims=True)
    hot = rank == lane
    perm = jnp.sum(jnp.where(hot, sub, 0), axis=0, keepdims=True)
    other_row = jnp.sum(jnp.where(hot, other_col, 0), axis=0, keepdims=True)
    keep = jnp.sum(jnp.where(hot & (rank != less), 1, 0), axis=0, keepdims=True)
    count = jnp.sum(jnp.where(key_col <= lane, 1, 0), axis=0, keepdims=True)
    has = jnp.sum(jnp.where(key_col == lane, 1, 0), axis=0, keepdims=True)
    return [perm, other_row, keep, jnp.maximum(count - 1, 0), has]


def kernel(
    feat_h, weight_h, bias_v, cot_h, idx_v, hub_v, low_h, hubt_h, ls_v, ld_v, hs_v, hd_v,
    out_h, fg_h, wg_o, bg_o,
    feat, weight, cot, tile_f, tile_b, table_v, table, xs, sbuf, lowr, hub_a, hub_b,
    own_hub, x_low, x_hub, seg, zsum, sumf, cotf, biasb, biasf, s_hi, s_lo, w_hi, w_lo,
    t_hi, t_lo, p_hi, p_lo, outc, gsend, gradf, x_grad, bbuf, backr, hpart, hcore, hsum,
    r_a, r_b, t_a, t_b, q_a, q_b, wgs, wzr, w1, wcr, w2, wxr, w3, wyr, wfin, acc,
    lsem, ss, rs,
):
    me = lax.axis_index("dom")
    z = lax.axis_index("rep")
    x, y, c = me // 8, lax.rem(me // 2, 4), lax.rem(me, 2)

    def dev(px, py, pc):
        return (lax.rem(px, 4) * 4 + lax.rem(py, 4)) * 2 + pc

    def at_x(d):
        return {"dom": dev(x + d, y, c), "rep": z}

    def at_y(d):
        return {"dom": dev(x, y + d, c), "rep": z}

    def at_z(d):
        return {"dom": me, "rep": lax.rem(z + d, 4)}

    at_core = {"dom": dev(x, y, 1 - c), "rep": z}

    def remote(src, dst, sem, target):
        return pltpu.make_async_remote_copy(
            src_ref=src, dst_ref=dst, send_sem=ss.at[sem], recv_sem=rs.at[sem],
            device_id=target, device_id_type=MESH,
        )

    started = []

    def send(src, dst, sem, target):
        copy = remote(src, dst, sem, target)
        copy.start()
        started.append(copy)
        return copy

    loads = [
        pltpu.make_async_copy(s, d, lsem.at[i])
        for i, (s, d) in enumerate(
            [(feat_h, feat), (cot_h, cot), (weight_h, weight),
             (low_h, tile_f.at[pl.ds(0, LT)]), (hubt_h, tile_f.at[pl.ds(LT, HT)])]
        )
    ]
    for load in loads:
        load.start()

    barrier = pltpu.get_barrier_semaphore()

    def greet(i, _):
        other = lax.rem(me + i, 32)
        pl.semaphore_signal(barrier, inc=1, device_id={"dom": other, "rep": z}, device_id_type=MESH)
        return 0

    lax.fori_loop(1, 32, greet, 0)
    for d in (1, 2, 3):
        pl.semaphore_signal(barrier, inc=1, device_id=at_z(d), device_id_type=MESH)

    loads[0].wait()
    high, low = split(feat[...])
    xs[0:FL] = high
    xs[FL:] = low
    own_hub[...] = fold(mm(xs[...], place(hub_v[...]), NN))
    hub_a[x, y, c] = own_hub[0:32]
    hub_b[x, y, c] = own_hub[32:64]
    biasb[...] = bias_v[...]
    pl.semaphore_wait(barrier, 34)

    hub1 = []
    for d in (2, 1, 3):
        hub1.append(send(hub_a.at[x, y, c], hub_a.at[x, y, c], HUB1A + d - 1, at_x(d)))
        hub1.append(send(hub_b.at[x, y, c], hub_b.at[x, y, c], HUB1B + d - 1, at_y(d)))

    def chip(j):
        jj = j + jnp.where(j >= 10, 1, 0)
        return lax.rem(2 + lax.rem(jj, 4), 4), lax.rem(2 + jj // 4, 4)

    def gather_pair(first):
        idx = jnp.concatenate([idx_v[pl.ds(first, 1), :], idx_v[pl.ds(first + 1, 1), :]], axis=1)
        return fold(mm(xs[...], place(idx), NN))

    def slot(dx, dy, tc):
        return (dx * 4 + dy) * 2 + lax.rem(tc + c, 2)

    def send_low(j, _):
        dx, dy = chip(j)
        first = dev(x + dx, y + dy, 0)
        rows = gather_pair(first)
        for tc in (0, 1):
            k = slot(dx, dy, tc)
            sbuf[k] = rows[:, tc * B : (tc + 1) * B]
            remote(sbuf.at[k], lowr.at[me], LOW + k, {"dom": first + tc, "rep": z}).start()
        return 0

    lax.fori_loop(0, 6, send_low, 0)

    for copy in hub1:
        copy.wait_recv()
    hub2 = []
    for d in (2, 1, 3):
        hub2.append(send(hub_a.at[:, y, c], hub_a.at[:, y, c], HUB2A + d - 1, at_y(d)))
        hub2.append(send(hub_b.at[x, :, c], hub_b.at[x, :, c], HUB2B + d - 1, at_x(d)))

    lax.fori_loop(6, 15, send_low, 0)
    rows = gather_pair(dev(x, y, 0))
    first_half, second_half = rows[:, :B], rows[:, B:]
    lowr[me] = jnp.where(c == 0, first_half, second_half)
    sbuf[1] = jnp.where(c == 0, second_half, first_half)
    send(sbuf.at[1], lowr.at[me], LOW + 1, at_core)

    loads[1].wait()
    cots = []
    for d in (2, 1, 3):
        other = lax.rem(z + d, 4)
        cots.append(
            send(cot.at[:, pl.ds(pl.multiple_of(other * CH, CH), CH)], cotf.at[z], COT + d - 1, at_z(d))
        )
        cots.append(send(biasb, biasf.at[z], BIAS + d - 1, at_z(d)))
    cotf[z] = cot[:, pl.ds(pl.multiple_of(z * CH, CH), CH)]
    biasf[z] = biasb[...]

    keys = [(ld_v, ls_v), (hd_v, hs_v), (ls_v, ld_v), (hs_v, hd_v)]
    for i, (a, b) in enumerate(keys):
        for r, row in enumerate(order(a[...], b[...])):
            table_v[i * 8 + r : i * 8 + r + 1, 0 : row.shape[1]] = row
    to_scalars = pltpu.make_async_copy(table_v, table, lsem.at[5])
    to_scalars.start()

    loads[2].wait()
    w = weight[...]
    wt = jnp.transpose(w)
    high, low = split(w)
    w_hi[...] = high.reshape(4, FL, 256)
    w_lo[...] = low.reshape(4, FL, 256)
    high, low = split(wt)
    t_hi[...] = high.reshape(4, FL, 256)
    t_lo[...] = low.reshape(4, FL, 256)

    loads[3].wait()
    loads[4].wait()

    def convert(g, _):
        for u in range(4):
            t = g * 4 + u
            h, l = split(tile_f[t])
            tile_b[t, 0] = h
            tile_b[t, 1] = l
        return 0

    lax.fori_loop(0, (LT + HT) // 4, convert, 0)
    to_scalars.wait()

    for copy in hub2:
        copy.wait_recv()
    hub3 = [
        send(hub_a.at[:, :, c], hub_a.at[:, :, c], HUB3, at_core),
        send(hub_b.at[:, :, c], hub_b.at[:, :, c], HUB3 + 1, at_core),
    ]
    for copy in hub3:
        copy.wait_recv()

    def tiles(which, count, base, source, forward):
        row = which * 8

        def step(g, total):
            parts = []
            for u in range(UNROLL):
                t = g * UNROLL + u
                p = jnp.clip(table[row, t], 0, count - 1)
                s = jnp.clip(table[row + 1, t], 0, source.shape[0] - 1)
                if forward:
                    r = mm(source[s], tile_b[base + p].reshape(2 * B, B), NT)
                else:
                    pair = tile_b[base + p]
                    r = mm(source[s], jnp.concatenate([pair[0], pair[1]], axis=1), NN)
                r = fold(r)
                parts.append(r[:, :B] + r[:, B:])
            for u in range(UNROLL):
                t = g * UNROLL + u
                total = parts[u] + jnp.where(table[row + 2, t] == 0, 0.0, total)
                seg[base + t] = total
            return total

        lax.fori_loop(0, count // UNROLL, step, jnp.zeros((FL, B), F32))

    def block(which, base, b):
        found = seg[base + jnp.clip(table[which * 8 + 3, b], 0, (HT if base else LT) - 1)]
        return jnp.where(table[which * 8 + 4, b] == 0, 0.0, found)

    def split_hub(i, _):
        ix, iy, ic = i // 8, lax.rem(i // 2, 4), lax.rem(i, 2)
        h, l = split(hub_a[ix, iy, ic])
        x_hub[i, 0:32] = h
        x_hub[i, 64:96] = l
        h, l = split(hub_b[ix, iy, ic])
        x_hub[i, 32:64] = h
        x_hub[i, 96:128] = l
        return 0

    lax.fori_loop(0, 32, split_hub, 0)
    tiles(1, HT, LT, x_hub, True)

    def take_low(j, _):
        dx, dy = chip(j)
        first = dev(x + 4 - dx, y + 4 - dy, 0)
        for sc in (0, 1):
            k = slot(dx, dy, sc)
            remote(sbuf.at[k], lowr.at[first + sc], LOW + k, at_core).wait_recv()
            h, l = split(lowr[first + sc])
            x_low[first + sc, 0:FL] = h
            x_low[first + sc, FL:] = l
        return 0

    lax.fori_loop(0, 15, take_low, 0)
    remote(sbuf.at[1], lowr.at[me], LOW + 1, at_core).wait_recv()
    first = dev(x, y, 0)
    for sc in (0, 1):
        h, l = split(lowr[first + sc])
        x_low[first + sc, 0:FL] = h
        x_low[first + sc, FL:] = l
    tiles(0, LT, 0, x_low, True)

    def sums(zc, put):
        for i in range(4):
            b = zc * 4 + i
            put(i, block(0, 0, b) + block(1, LT, b))

    swaps = []
    for d in (2, 1, 3):

        def put(i, value, d=d):
            zsum[d, :, i * B : (i + 1) * B] = value

        sums(lax.rem(z + d, 4), put)
        swaps.append(send(zsum.at[d], sumf.at[z], SUM + d - 1, at_z(d)))

    def put_own(i, value):
        sumf[z, :, i * B : (i + 1) * B] = value

    sums(z, put_own)
    for copy in cots + swaps:
        copy.wait_recv()

    high, low = split(sumf[...])
    s_hi[...] = high
    s_lo[...] = low

    def dense(zc, _):
        r = fold(mm(jnp.concatenate([t_hi[zc], t_lo[zc]], axis=0), s_hi[...].reshape(256, CH), NN))
        r = r + mm(t_hi[zc], s_lo[...].reshape(256, CH), NN)
        bias = biasf[zc]
        pre = r + jnp.concatenate([bias] * 4, axis=1)
        sig = jax.nn.sigmoid(pre)
        outc[zc] = pre * sig
        grad = cotf[zc] * sig * (1.0 + pre * (1.0 - sig))
        h, l = split(grad)
        p_hi[zc] = h
        p_lo[zc] = l
        return 0

    lax.fori_loop(0, 4, dense, 0)

    def back_rows(zc):
        both = jnp.concatenate([w_hi[zc], w_lo[zc]], axis=0)
        r = fold(mm(both, p_hi[...].reshape(256, CH), NN))
        return r + mm(w_hi[zc], p_lo[...].reshape(256, CH), NN)

    grads = []
    for d in (2, 1, 3):
        gsend[d] = back_rows(lax.rem(z + d, 4))
        grads.append(send(gsend.at[d], gradf.at[z], GRAD + d - 1, at_z(d)))
    gradf[z] = back_rows(z)

    def out_part():
        return out_h.at[:, pl.ds(pl.multiple_of(z * CH, CH), CH)]

    outs = []
    for d in (2, 1, 3):
        outs.append(send(outc.at[lax.rem(z + d, 4)], out_part(), OUT + d - 1, at_z(d)))
    own_out = pltpu.make_async_copy(outc.at[z], out_part(), lsem.at[6])
    own_out.start()

    def weight_rows(zc, _):
        both = jnp.concatenate([s_hi[zc], s_lo[zc]], axis=0)
        r = fold(mm(both, p_hi[...].reshape(256, CH), NT))
        r = r + mm(s_hi[zc], p_lo[...].reshape(256, CH), NT)
        ones = jnp.ones((16, CH), BF16)
        bsum = mm(ones, p_hi[...].reshape(256, CH), NT) + mm(ones, p_lo[...].reshape(256, CH), NT)
        wgs[zc, 0:FL] = r
        wgs[zc, FL:] = bsum[0:8]
        return 0

    lax.fori_loop(0, 4, weight_rows, 0)
    wz = [send(wgs.at[lax.rem(z + d, 4)], wzr.at[d - 1], WZ + d - 1, at_z(d)) for d in (2, 1, 3)]

    for copy in grads:
        copy.wait_recv()
    for b in range(NB):
        h, l = split(gradf[b // 4, :, (b % 4) * B : (b % 4 + 1) * B])
        x_grad[b, 0:FL] = h
        x_grad[b, FL:] = l
    tiles(2, LT, 0, x_grad, False)

    def send_back(j, _):
        dx, dy = chip(j)
        first = dev(x + dx, y + dy, 0)
        for tc in (0, 1):
            k = slot(dx, dy, tc)
            bbuf[k] = block(2, 0, first + tc)
            remote(bbuf.at[k], backr.at[me], BACK + k, {"dom": first + tc, "rep": z}).start()
        return 0

    lax.fori_loop(0, 15, send_back, 0)
    bbuf[1] = block(2, 0, dev(x, y, 1 - c))
    send(bbuf.at[1], backr.at[me], BACK + 1, at_core)
    backr[me] = block(2, 0, me)

    tiles(3, HT, LT, x_grad, False)

    def hub_blocks(i, _):
        hpart[i // 8, lax.rem(i // 2, 4), lax.rem(i, 2)] = block(3, LT, i)
        return 0

    lax.fori_loop(0, 32, hub_blocks, 0)
    red0 = send(hpart.at[:, :, 1 - c], hcore, RED0, at_core)

    for copy in wz:
        copy.wait_recv()
    total = wgs[z] + wzr[0] + wzr[1] + wzr[2]
    w1[0] = total[:, :B]
    w1[1] = total[:, B:]
    wc = send(w1.at[1 - c], wcr, WC, at_core)

    red0.wait_recv()
    hsum[...] = hpart[:, :, c] + hcore[...]
    red1 = []
    for d in (2, 1, 3):
        src = hsum.at[lax.rem(x + d, 4), :, pl.ds(0, 32)]
        red1.append(send(src, r_a.at[d - 1], RED1A + d - 1, at_x(d)))
        src = hsum.at[:, lax.rem(y + d, 4), pl.ds(32, 32)]
        red1.append(send(src, r_b.at[d - 1], RED1B + d - 1, at_y(d)))

    wc.wait_recv()
    w2[...] = w1[c] + wcr[...]
    wx = [send(w2, wxr.at[d - 1], WX + d - 1, at_x(d)) for d in (2, 1, 3)]

    acc[...] = jnp.zeros((FL, VD), F32)

    def add_pair(first):
        idx = jnp.concatenate([idx_v[pl.ds(first, 1), :], idx_v[pl.ds(first + 1, 1), :]], axis=1)
        h, l = split(jnp.concatenate([backr[first], backr[first + 1]], axis=1))
        acc[...] += fold(mm(jnp.concatenate([h, l], axis=0), place(idx), NT))

    def take_back(j, _):
        dx, dy = chip(j)
        first = dev(x + 4 - dx, y + 4 - dy, 0)
        for sc in (0, 1):
            k = slot(dx, dy, sc)
            remote(bbuf.at[k], backr.at[first + sc], BACK + k, at_core).wait_recv()
        add_pair(first)
        return 0

    remote(bbuf.at[1], backr.at[me], BACK + 1, at_core).wait_recv()
    add_pair(dev(x, y, 0))
    lax.fori_loop(0, 5, take_back, 0)

    for copy in wx:
        copy.wait_recv()
    w3[...] = w2[...] + wxr[0] + wxr[1] + wxr[2]
    wy = [send(w3, wyr.at[d - 1], WY + d - 1, at_y(d)) for d in (2, 1, 3)]

    lax.fori_loop(5, 10, take_back, 0)

    for copy in red1:
        copy.wait_recv()
    t_a[...] = hsum[x, :, 0:32] + r_a[0] + r_a[1] + r_a[2]
    t_b[...] = hsum[:, y, 32:64] + r_b[0] + r_b[1] + r_b[2]
    red2 = []
    for d in (2, 1, 3):
        red2.append(send(t_a.at[lax.rem(y + d, 4)], q_a.at[d - 1], RED2A + d - 1, at_y(d)))
        red2.append(send(t_b.at[lax.rem(x + d, 4)], q_b.at[d - 1], RED2B + d - 1, at_x(d)))

    for copy in wy:
        copy.wait_recv()
    wfin[c] = w3[...] + wyr[0] + wyr[1] + wyr[2]
    wc2 = send(wfin.at[c], wfin.at[c], WC2, at_core)

    lax.fori_loop(10, 15, take_back, 0)

    for copy in red2:
        copy.wait_recv()
    h_a, l_a = split(t_a[y] + q_a[0] + q_a[1] + q_a[2])
    h_b, l_b = split(t_b[x] + q_b[0] + q_b[1] + q_b[2])
    both = jnp.concatenate([h_a, h_b, l_a, l_b], axis=0)
    acc[...] += fold(mm(both, place(hub_v[...]), NT))
    store = pltpu.make_async_copy(acc, fg_h, lsem.at[7])
    store.start()

    wc2.wait_recv()
    scale = 1.0 / math.sqrt(VD * 32)
    wg_o[:, :B] = wfin[0, 0:FL] * scale
    wg_o[:, B:] = wfin[1, 0:FL] * scale
    row = jnp.concatenate([wfin[0, FL : FL + 1], wfin[1, FL : FL + 1]], axis=1)
    mine = jnp.zeros((1, FL), F32)
    for i in range(4):
        mine = mine + jnp.where(z == i, row[:, i * FL : (i + 1) * FL], 0.0)
    bg_o[...] = mine * scale

    for copy in outs:
        copy.wait_recv()
    own_out.wait()
    store.wait()

    def drain(k, _):
        remote(sbuf.at[k], lowr.at[me], LOW + k, at_core).wait_send()
        remote(bbuf.at[k], backr.at[me], BACK + k, at_core).wait_send()
        return 0

    lax.fori_loop(2, 32, drain, 0)
    for copy in started:
        copy.wait_send()


def vm(shape, dtype=F32):
    return pltpu.VMEM(shape, dtype)


SCRATCH = [
    vm((FL, VD)), vm((256, 256)), vm((FL, VD)), vm((LT + HT, B, B)),
    vm((LT + HT, 2, B, B), BF16), vm((32, B), I32), pltpu.SMEM((32, B), I32),
    vm((2 * FL, VD), BF16), vm((32, FL, B)), vm((32, FL, B)),
    vm((4, 4, 2, 32, B)), vm((4, 4, 2, 32, B)),
    vm((FL, B)), vm((32, 2 * FL, B), BF16), vm((32, 2 * FL, B), BF16), vm((LT + HT, FL, B)),
    vm((4, FL, CH)), vm((4, FL, CH)), vm((4, FL, CH)), vm((FL, B)), vm((4, FL, B)),
    vm((4, FL, CH), BF16), vm((4, FL, CH), BF16), vm((4, FL, 256), BF16), vm((4, FL, 256), BF16),
    vm((4, FL, 256), BF16), vm((4, FL, 256), BF16), vm((4, FL, CH), BF16), vm((4, FL, CH), BF16),
    vm((4, FL, CH)), vm((4, FL, CH)), vm((4, FL, CH)), vm((NB, 2 * FL, B), BF16),
    vm((32, FL, B)), vm((32, FL, B)), vm((4, 4, 2, FL, B)), vm((4, 4, FL, B)), vm((4, 4, FL, B)),
    vm((3, 4, 32, B)), vm((3, 4, 32, B)), vm((4, 32, B)), vm((4, 32, B)),
    vm((3, 32, B)), vm((3, 32, B)), vm((4, 72, 256)), vm((3, 72, 256)), vm((2, 72, B)),
    vm((72, B)), vm((72, B)), vm((3, 72, B)), vm((72, B)), vm((3, 72, B)), vm((2, 72, B)),
    vm((FL, VD)),
    pltpu.SemaphoreType.DMA((8,)), pltpu.SemaphoreType.DMA((NSEM,)),
    pltpu.SemaphoreType.DMA((NSEM,)),
]


def shards(
    features, weight, bias, cotangent, send_index, send_count, hub_local,
    low_tiles, low_src, low_dst, hub_tiles, hub_src, hub_dst,
):
    lanes = jnp.arange(B, dtype=I32)
    idx = jnp.where(lanes[None, :] < send_count[0][:, None], send_index.reshape(32, B), -1)
    bias_block = jnp.broadcast_to(bias[:, None], (FL, B))
    hbm = pl.BlockSpec(memory_space=pl.ANY)
    vmem = pl.BlockSpec(memory_space=pltpu.VMEM)
    out, fg, wg, bg = pl.pallas_call(
        kernel,
        out_shape=(
            jax.ShapeDtypeStruct((FL, VD), F32),
            jax.ShapeDtypeStruct((FL, VD), F32),
            jax.ShapeDtypeStruct((FL, 256), F32),
            jax.ShapeDtypeStruct((1, FL), F32),
        ),
        in_specs=[hbm, hbm, vmem, hbm, vmem, vmem, hbm, hbm, vmem, vmem, vmem, vmem],
        out_specs=(hbm, hbm, vmem, vmem),
        scratch_shapes=SCRATCH,
        compiler_params=pltpu.CompilerParams(
            collective_id=0, has_side_effects=True, vmem_limit_bytes=60 * 2**20
        ),
        cost_estimate=pl.CostEstimate(
            flops=4 * 10**9, bytes_accessed=16 * 2**20, transcendentals=131072
        ),
    )(
        features, weight, bias_block, cotangent, idx, hub_local[None, :], low_tiles, hub_tiles,
        low_src[None, :], low_dst[None, :], hub_src[None, :], hub_dst[None, :],
    )
    return out, fg, wg, bg[0]


def solution(mesh):
    return jax.shard_map(
        shards,
        mesh=mesh,
        in_specs=(
            P("rep", "dom"),
            P(),
            P("rep"),
            P("rep", "dom"),
            P("dom", None),
            P("dom", None),
            P("dom"),
            P("dom", None, None),
            P("dom"),
            P("dom"),
            P("dom", None, None),
            P("dom"),
            P("dom"),
        ),
        out_specs=(P("rep", "dom"), P("rep", "dom"), P("rep", None), P("rep")),
        check_vma=False,
    )
```

```python
import math

import jax
import jax.numpy as jnp
from jax import lax
from jax.experimental import pallas as pl
from jax.experimental.pallas import tpu as pltpu
from jax.sharding import PartitionSpec as P

F32 = jnp.float32
BF16 = jnp.bfloat16
I32 = jnp.int32
NN = (((1,), (0,)), ((), ()))
NT = (((1,), (1,)), ((), ()))
MESH = pl.DeviceIdType.MESH

FL = 64
VD = 2048
CH = 512
B = 128
LT, HT = 128, 64
NB = 16
UNROLL = 32

OFFSETS = sorted(
    [(i, j, k) for i in range(4) for j in range(4) for k in range(2) if (i, j, k) != (0, 0, 0)],
    key=lambda o: (-min(o[0], 4 - o[0]) - min(o[1], 4 - o[1]), o[2]),
)
CHIPS = [(i, j) for i, j, k in OFFSETS if k == 0]
CHIPS_X = sum(i << (2 * n) for n, (i, j) in enumerate(CHIPS))
CHIPS_Y = sum(j << (2 * n) for n, (i, j) in enumerate(CHIPS))
FIRST = 14
H = FL // 2

LOW, BACK = (0, 1, 2), ((3, 4, 5), (6, 7, 8))
COT, SUM, GRAD, OUT, WZ = 9, (10, 11), (12, 13), 14, 15
HUB1, HUB2, HUB3, RED0, RED1, RED2, WC, WX, WY, WC2 = range(16, 26)
NSEM = 26


def mm(a, b, dims):
    return lax.dot_general(a, b, dims, preferred_element_type=F32)


def split(x):
    high = x.astype(BF16)
    return high, (x - high.astype(F32)).astype(BF16)


def fold(r):
    return r[:FL] + r[FL:]


def place(idx):
    return (lax.broadcasted_iota(I32, (VD, idx.shape[1]), 0) == idx).astype(BF16)


def place_t(col):
    lanes = lax.broadcasted_iota(I32, (col.shape[0], VD), 1)
    return (lanes == jnp.concatenate([col] * (VD // B), axis=1)).astype(BF16)


def halves(r):
    parts = [r[i : i + H] + r[i + H : i + 2 * H] for i in range(0, r.shape[0], 2 * H)]
    return parts[0] if len(parts) == 1 else jnp.concatenate(parts, axis=0)


def split_into(ref, i, half, value):
    high, low = split(value)
    ref[i, 2 * H * half : 2 * H * half + H] = high
    ref[i, 2 * H * half + H : 2 * H * half + 2 * H] = low


def order(key, other):
    n = key.shape[1]
    lane = lax.broadcasted_iota(I32, (n, n), 1)
    sub = lax.broadcasted_iota(I32, (n, n), 0)
    eye = lane == sub
    key = jnp.broadcast_to(key, (n, n))
    other = jnp.broadcast_to(other, (n, n))
    key_col = jnp.sum(jnp.where(eye, key, 0), axis=1, keepdims=True)
    other_col = jnp.sum(jnp.where(eye, other, 0), axis=1, keepdims=True)
    less = jnp.sum(jnp.where(key < key_col, 1, 0), axis=1, keepdims=True)
    before = (key == key_col) & (lane < sub)
    rank = less + jnp.sum(jnp.where(before, 1, 0), axis=1, keepdims=True)
    hot = rank == lane
    perm = jnp.sum(jnp.where(hot, sub, 0), axis=0, keepdims=True)
    other_row = jnp.sum(jnp.where(hot, other_col, 0), axis=0, keepdims=True)
    keep = jnp.sum(jnp.where(hot & (rank != less), 1, 0), axis=0, keepdims=True)
    count = jnp.sum(jnp.where(key_col <= lane, 1, 0), axis=0, keepdims=True)
    has = jnp.sum(jnp.where(key_col == lane, 1, 0), axis=0, keepdims=True)
    return [perm, other_row, keep, jnp.maximum(count - 1, 0), has]


def kernel(
    feat_h, weight_h, bias_v, cot_h, index_v, count_v, hub_v, low_h, hubt_h, ls_v, ld_v, hs_v, hd_v,
    out_h, fg_h, wg_o, bg_o,
    idx_v, idx_c, hub_c, feat, weight, cot, tile_f, tile_b, tile_t, table_v, table, xs, sbuf, lowr,
    hub_a, hub_b, own_hub, x_low, x_hub, seg, hseg, zsum, sumf, cotf, biasb, biasf, s_hi, s_lo,
    w_hi, w_lo, t_hi, t_lo, p_hi, p_lo, outc, gsend, gradf, x_grad, bbuf, backr, hpart, hcore, hsum,
    r_a, r_b, t_a, t_b, q_a, q_b, wgs, wzr, w1, wcr, w2, wxr, w3, wyr, wfin, acc,
    lsem, ss, rs,
):
    me = lax.axis_index("dom")
    z = lax.axis_index("rep")
    x, y, c = me // 8, lax.rem(me // 2, 4), lax.rem(me, 2)

    def dev(px, py, pc):
        return (lax.rem(px, 4) * 4 + lax.rem(py, 4)) * 2 + pc

    def at_x(d):
        return {"dom": dev(x + d, y, c), "rep": z}

    def at_y(d):
        return {"dom": dev(x, y + d, c), "rep": z}

    def at_z(d):
        return {"dom": me, "rep": lax.rem(z + d, 4)}

    at_core = {"dom": dev(x, y, 1 - c), "rep": z}

    def remote(src, dst, sem, target):
        return pltpu.make_async_remote_copy(
            src_ref=src, dst_ref=dst, send_sem=ss.at[sem], recv_sem=rs.at[sem],
            device_id=target, device_id_type=MESH,
        )

    sent = {}

    def unit(n):
        return lowr.at[pl.ds(0, n), pl.ds(0, H)]

    def send(src, dst, sem, target):
        remote(src, dst, sem, target).start()
        sent.setdefault(sem, []).append(math.prod(src.shape))

    def size(sem):
        total = sum(sent[sem])
        if sem == WZ:
            return wzr
        if sem in (WX, WY):
            return wxr
        if sem in (WC, WC2):
            return wcr
        return unit(total // (H * B))

    def arrived(sem):
        remote(size(sem), size(sem), sem, at_core).wait_recv()

    loads = [
        pltpu.make_async_copy(s, d, lsem.at[i])
        for i, (s, d) in enumerate(
            [(feat_h, feat), (cot_h, cot), (weight_h, weight),
             (low_h, tile_f), (hubt_h, tile_f.at[pl.ds(0, HT)])]
        )
    ]
    for load in loads[:4]:
        load.start()

    barrier = pltpu.get_barrier_semaphore()

    def greet(i, _):
        other = lax.rem(me + i, 32)
        pl.semaphore_signal(barrier, inc=1, device_id={"dom": other, "rep": z}, device_id_type=MESH)
        return 0

    lax.fori_loop(1, 32, greet, 0)
    for d in (1, 2, 3):
        pl.semaphore_signal(barrier, inc=1, device_id=at_z(d), device_id_type=MESH)

    lane = lax.broadcasted_iota(I32, (32, B), 1)
    sub = lax.broadcasted_iota(I32, (32, 32), 0)
    eye = sub == lax.broadcasted_iota(I32, (32, 32), 1)
    count = jnp.broadcast_to(count_v[...], (32, 32))
    count = jnp.sum(jnp.where(eye, count, 0), axis=1, keepdims=True)
    idx_v[...] = jnp.where(lane < count, index_v[...], -1)
    eye = lax.broadcasted_iota(I32, (FL, FL), 0) == lax.broadcasted_iota(I32, (FL, FL), 1)
    bias = jnp.where(eye, jnp.broadcast_to(bias_v[...], (FL, FL)), 0.0)
    biasb[...] = jnp.broadcast_to(jnp.sum(bias, axis=1, keepdims=True), (FL, B))

    loads[0].wait()
    high, low = split(feat[...])
    xs[0:FL] = high
    xs[FL:] = low
    own_hub[...] = fold(mm(xs[...], place(hub_v[...]), NN))
    hub_a[x, y, c] = own_hub[0:32]
    hub_b[x, y, c] = own_hub[32:64]

    def gather_pair(i, _):
        idx = jnp.concatenate([idx_v[pl.ds(2 * i, 1), :], idx_v[pl.ds(2 * i + 1, 1), :]], axis=1)
        rows = fold(mm(xs[...], place(idx), NN))
        sbuf[2 * i] = rows[:, :B]
        sbuf[2 * i + 1] = rows[:, B:]
        return 0

    lax.fori_loop(0, 16, gather_pair, 0)
    lowr[me] = sbuf[me]
    pl.semaphore_wait(barrier, 34)

    for d in (2, 1, 3):
        send(hub_a.at[x, y, c], hub_a.at[x, y, c], HUB1, at_x(d))
        send(hub_b.at[x, y, c], hub_b.at[x, y, c], HUB1, at_y(d))

    def rows_of(half):
        return pl.ds(half * H, H)

    def exchange(src, dst, half, group, begin=0, end=31):
        part = rows_of(half)
        for dx, dy, dc in OFFSETS[begin:end]:
            to = dev(x + dx, y + dy, lax.rem(c + dc, 2))
            sem = group(dx, dy)
            send(src.at[to, part], dst.at[me, part], sem, {"dom": to, "rep": z})

    def chip(j):
        return (CHIPS_X >> (2 * j)) & 3, (CHIPS_Y >> (2 * j)) & 3

    exchange(sbuf, lowr, 0, lambda dx, dy: LOW[0], 0, FIRST)

    arrived(HUB1)
    for d in (2, 1, 3):
        send(hub_a.at[:, y, c], hub_a.at[:, y, c], HUB2, at_y(d))
        send(hub_b.at[x, :, c], hub_b.at[x, :, c], HUB2, at_x(d))

    exchange(sbuf, lowr, 0, lambda dx, dy: LOW[1], FIRST, 31)

    loads[1].wait()
    for d in (2, 1, 3):
        other = lax.rem(z + d, 4)
        chunk = pl.ds(pl.multiple_of(other * CH, CH), CH)
        send(cot.at[:, chunk], cotf.at[z], COT, at_z(d))
        send(biasb, biasf.at[z], COT, at_z(d))
    cotf[z] = cot[:, pl.ds(pl.multiple_of(z * CH, CH), CH)]
    biasf[z] = biasb[...]

    keys = [(ld_v, ls_v), (hd_v, hs_v), (ls_v, ld_v), (hs_v, hd_v)]
    for i, (a, b) in enumerate(keys):
        for r, row in enumerate(order(a[...], b[...])):
            table_v[i * 8 + r : i * 8 + r + 1, 0 : row.shape[1]] = row
    to_scalars = pltpu.make_async_copy(table_v, table, lsem.at[5])
    to_scalars.start()

    loads[2].wait()
    w = weight[...]
    wt = jnp.transpose(w)
    high, low = split(w)
    w_hi[...] = high.reshape(4, FL, 256)
    w_lo[...] = low.reshape(4, FL, 256)
    high, low = split(wt)
    t_hi[...] = high.reshape(4, FL, 256)
    t_lo[...] = low.reshape(4, FL, 256)

    square = lax.broadcasted_iota(I32, (B, B), 0) == lax.broadcasted_iota(I32, (B, B), 1)

    def column(row):
        picked = jnp.where(square, jnp.broadcast_to(row, (B, B)), 0)
        return jnp.broadcast_to(jnp.sum(picked, axis=1, keepdims=True), (B, B))

    def columns(i, _):
        idx_c[i] = column(idx_v[pl.ds(i, 1), :])
        return 0

    lax.fori_loop(0, 32, columns, 0)
    hub_c[...] = column(hub_v[...])

    def convert(base):
        def step(g, _):
            for u in range(4):
                t = g * 4 + u
                tile = tile_f[t]
                h, l = split(tile)
                tile_b[base + t, :, 0:B] = h
                tile_b[base + t, :, B:] = l
                h, l = split(jnp.transpose(tile))
                tile_t[base + t, :, 0:B] = h
                tile_t[base + t, :, B:] = l
            return 0

        return step

    arrived(LOW[0])
    exchange(sbuf, lowr, 1, lambda dx, dy: LOW[2])
    loads[3].wait()
    lax.fori_loop(0, HT // 4, convert(0), 0)
    loads[4].start()
    lax.fori_loop(HT // 4, LT // 4, convert(0), 0)
    to_scalars.wait()

    arrived(HUB2)
    send(hub_a.at[:, :, c], hub_a.at[:, :, c], HUB3, at_core)
    send(hub_b.at[:, :, c], hub_b.at[:, :, c], HUB3, at_core)
    loads[4].wait()
    lax.fori_loop(0, HT // 4, convert(LT), 0)

    def tiles(which, count, base, source, values, out):
        row = which * 8
        last_source = (NB if which >= 2 else 32) - 1

        def step(g, total):
            parts = []
            for u in range(UNROLL):
                t = g * UNROLL + u
                p = jnp.clip(table[row, t], 0, count - 1)
                s = jnp.clip(table[row + 1, t], 0, last_source)
                r = halves(mm(source(s), values[base + p], NN))
                parts.append(r[:, :B] + r[:, B:])
            for u in range(UNROLL):
                t = g * UNROLL + u
                total = parts[u] + jnp.where(table[row + 2, t] == 0, 0.0, total)
                out[t] = total
            return total

        lax.fori_loop(0, count // UNROLL, step, jnp.zeros(out.shape[1:], F32))

    def block(which, ref, b):
        found = ref[jnp.clip(table[which * 8 + 3, b], 0, ref.shape[0] - 1)]
        return jnp.where(table[which * 8 + 4, b] == 0, 0.0, found)

    def half_of(ref, half):
        return lambda s: ref[s, 2 * H * half : 2 * H * (half + 1)]

    def take_low(half):
        for sem in (LOW[2:], LOW[1:2])[half == 0]:
            arrived(sem)

        def split_low(g, _):
            for u in range(4):
                split_into(x_low, g * 4 + u, half, lowr[g * 4 + u, half * H : half * H + H])
            return 0

        lax.fori_loop(0, 8, split_low, 0)
        tiles(0, LT, 0, half_of(x_low, half), tile_t, seg)

    def split_hub(g, _):
        for u in range(4):
            i = g * 4 + u
            ix, iy, ic = i // 8, lax.rem(i // 2, 4), lax.rem(i, 2)
            split_into(x_hub, i, 0, hub_a[ix, iy, ic])
            split_into(x_hub, i, 1, hub_b[ix, iy, ic])
        return 0

    def sums(half):
        part = rows_of(half)

        def value(b):
            hub = jnp.where(table[12, b] == 0, 0.0, hseg[jnp.clip(table[11, b], 0, HT - 1), part])
            return block(0, seg, b) + hub

        for d in (2, 1, 3):
            for i in range(4):
                zsum[d, part, i * B : (i + 1) * B] = value(lax.rem(z + d, 4) * 4 + i)
            send(zsum.at[d, part], sumf.at[z, part], SUM[half], at_z(d))
        for i in range(4):
            sumf[z, part, i * B : (i + 1) * B] = value(z * 4 + i)

    arrived(HUB3)
    lax.fori_loop(0, 8, split_hub, 0)
    tiles(1, HT, LT, lambda s: x_hub[s], tile_t, hseg)
    take_low(0)
    sums(0)
    take_low(1)
    sums(1)
    for sem in (COT, SUM[0], SUM[1]):
        arrived(sem)

    high, low = split(sumf[...])
    s_hi[...] = high
    s_lo[...] = low

    def dense(zc, _):
        r = fold(mm(jnp.concatenate([t_hi[zc], t_lo[zc]], axis=0), s_hi[...].reshape(256, CH), NN))
        r = r + mm(t_hi[zc], s_lo[...].reshape(256, CH), NN)
        bias = biasf[zc]
        pre = r + jnp.concatenate([bias] * 4, axis=1)
        sig = jax.nn.sigmoid(pre)
        outc[zc] = pre * sig
        grad = cotf[zc] * sig * (1.0 + pre * (1.0 - sig))
        h, l = split(grad)
        p_hi[zc] = h
        p_lo[zc] = l
        return 0

    lax.fori_loop(0, 4, dense, 0)

    def back_rows(zc):
        both = jnp.concatenate([w_hi[zc], w_lo[zc]], axis=0)
        r = fold(mm(both, p_hi[...].reshape(256, CH), NN))
        return r + mm(w_hi[zc], p_lo[...].reshape(256, CH), NN)

    def send_grad(half, d):
        part = rows_of(half)
        send(gsend.at[d, part], gradf.at[z, part], GRAD[half], at_z(d))

    for d in (2, 1, 3):
        gsend[d] = back_rows(lax.rem(z + d, 4))
        send_grad(0, d)
    for d in (2, 1, 3):
        send_grad(1, d)
    gradf[z] = back_rows(z)

    def out_part():
        return out_h.at[:, pl.ds(pl.multiple_of(z * CH, CH), CH)]

    def weight_rows(zc, _):
        both = jnp.concatenate([s_hi[zc], s_lo[zc]], axis=0)
        r = fold(mm(both, p_hi[...].reshape(256, CH), NT))
        r = r + mm(s_hi[zc], p_lo[...].reshape(256, CH), NT)
        ones = jnp.ones((16, CH), BF16)
        bsum = mm(ones, p_hi[...].reshape(256, CH), NT) + mm(ones, p_lo[...].reshape(256, CH), NT)
        wgs[zc, 0:FL] = r
        wgs[zc, FL:] = bsum[0:8]
        return 0

    lax.fori_loop(0, 4, weight_rows, 0)
    for d in (2, 1, 3):
        send(wgs.at[lax.rem(z + d, 4)], wzr.at[d - 1], WZ, at_z(d))

    for d in (2, 1, 3):
        send(outc.at[lax.rem(z + d, 4)], out_part(), OUT, at_z(d))
    own_out = pltpu.make_async_copy(outc.at[z], out_part(), lsem.at[6])
    own_out.start()


    def take_grad(half):
        arrived(GRAD[half])
        for b in range(NB):
            value = gradf[b // 4, half * H : half * H + H, (b % 4) * B : (b % 4 + 1) * B]
            split_into(x_grad, b, half, value)

    def low_blocks(half):
        tiles(2, LT, 0, half_of(x_grad, half), tile_b, seg)

        def put(g, _):
            for u in range(4):
                bbuf[g * 4 + u, half * H : half * H + H] = block(2, seg, g * 4 + u)
            return 0

        lax.fori_loop(0, 8, put, 0)
        backr[me, half * H : half * H + H] = bbuf[me, half * H : half * H + H]

    take_grad(0)
    low_blocks(0)

    def back_group(half):
        return lambda dx, dy: BACK[half][CHIPS.index((dx, dy)) // 5 if dx + dy > 0 else 2]

    exchange(bbuf, backr, 0, back_group(0))

    take_grad(1)
    tiles(3, HT, LT, lambda s: x_grad[s], tile_b, hseg)

    def hub_blocks(g, _):
        for u in range(4):
            i = g * 4 + u
            hpart[i // 8, lax.rem(i // 2, 4), lax.rem(i, 2)] = block(3, hseg, i)
        return 0

    lax.fori_loop(0, 8, hub_blocks, 0)
    send(hpart.at[:, :, 1 - c], hcore, RED0, at_core)
    low_blocks(1)

    arrived(RED0)
    hsum[...] = hpart[:, :, c] + hcore[...]
    for d in (2, 1, 3):
        src = hsum.at[lax.rem(x + d, 4), :, pl.ds(0, 32)]
        send(src, r_a.at[d - 1], RED1, at_x(d))
        src = hsum.at[:, lax.rem(y + d, 4), pl.ds(32, 32)]
        send(src, r_b.at[d - 1], RED1, at_y(d))
    exchange(bbuf, backr, 1, back_group(1))

    acc[...] = jnp.zeros((FL, VD), F32)

    def add_pair(half, first):
        part = slice(half * H, half * H + H)
        h, l = split(jnp.concatenate([backr[first, part], backr[first + 1, part]], axis=1))
        col = jnp.concatenate([idx_c[first], idx_c[first + 1]], axis=0)
        acc[part, :] += halves(mm(jnp.concatenate([h, l], axis=0), place_t(col), NN))

    def take_back(half, group):
        def step(j, _):
            dx, dy = chip(j)
            add_pair(half, dev(x + 4 - dx, y + 4 - dy, 0))
            return 0

        arrived(BACK[half][group])
        lax.fori_loop(group * 5, group * 5 + 5, step, 0)
        if group == 2:
            add_pair(half, dev(x, y, 0))

    take_back(0, 0)
    arrived(WZ)
    total = wgs[z] + wzr[0] + wzr[1] + wzr[2]
    w1[0] = total[:, :B]
    w1[1] = total[:, B:]
    send(w1.at[1 - c], wcr, WC, at_core)
    take_back(0, 1)
    arrived(WC)
    w2[...] = w1[c] + wcr[...]
    for d in (2, 1, 3):
        send(w2, wxr.at[d - 1], WX, at_x(d))
    take_back(0, 2)

    arrived(RED1)
    t_a[...] = hsum[x, :, 0:32] + r_a[0] + r_a[1] + r_a[2]
    t_b[...] = hsum[:, y, 32:64] + r_b[0] + r_b[1] + r_b[2]
    for d in (2, 1, 3):
        send(t_a.at[lax.rem(y + d, 4)], q_a.at[d - 1], RED2, at_y(d))
        send(t_b.at[lax.rem(x + d, 4)], q_b.at[d - 1], RED2, at_x(d))

    arrived(WX)
    w3[...] = w2[...] + wxr[0] + wxr[1] + wxr[2]
    for d in (2, 1, 3):
        send(w3, wyr.at[d - 1], WY, at_y(d))
    take_back(1, 0)
    take_back(1, 1)
    arrived(WY)
    wfin[c] = w3[...] + wyr[0] + wyr[1] + wyr[2]
    send(wfin.at[c], wfin.at[c], WC2, at_core)
    take_back(1, 2)

    arrived(RED2)
    h_a, l_a = split(t_a[y] + q_a[0] + q_a[1] + q_a[2])
    h_b, l_b = split(t_b[x] + q_b[0] + q_b[1] + q_b[2])
    both = jnp.concatenate([h_a, h_b, l_a, l_b], axis=0)
    acc[...] += fold(mm(both, place_t(hub_c[...]), NN))
    store = pltpu.make_async_copy(acc, fg_h, lsem.at[7])
    store.start()

    arrived(WC2)
    scale = 1.0 / math.sqrt(VD * 32)
    wg_o[:, :B] = wfin[0, 0:FL] * scale
    wg_o[:, B:] = wfin[1, 0:FL] * scale
    row = jnp.concatenate([wfin[0, FL : FL + 1], wfin[1, FL : FL + 1]], axis=1)
    mine = jnp.zeros((1, FL), F32)
    for i in range(4):
        mine = mine + jnp.where(z == i, row[:, i * FL : (i + 1) * FL], 0.0)
    bg_o[...] = mine * scale

    arrived(OUT)
    own_out.wait()
    store.wait()

    for sem in sent:
        remote(size(sem), size(sem), sem, at_core).wait_send()


def hand_over(a, b, c, d, out_a, out_b, out_c, out_d, va, vb, vc, vd, sem_in, sem_out):
    rows = [pl.ds(0, 32), pl.ds(32, 32)]
    trips = [(r.at[h], v.at[h], o.at[h]) for h in rows for r, v, o in [(a, va, out_a), (b, vb, out_b)]]
    trips += [(c, vc, out_c), (d, vd, out_d)]
    fetch = [pltpu.make_async_copy(r, v, sem_in.at[i]) for i, (r, v, _) in enumerate(trips)]
    store = [pltpu.make_async_copy(v, o, sem_out.at[i]) for i, (_, v, o) in enumerate(trips)]
    for copy in fetch:
        copy.start()
    for first, then in zip(fetch, store):
        first.wait()
        then.start()
    for copy in store:
        copy.wait()


def vm(shape, dtype=F32):
    return pltpu.VMEM(shape, dtype)


SCRATCH = [
    vm((32, B), I32), vm((32, B, B), I32), vm((B, B), I32),
    vm((FL, VD)), vm((256, 256)), vm((FL, VD)), vm((LT, B, B)),
    vm((LT + HT, B, 2 * B), BF16), vm((LT + HT, B, 2 * B), BF16),
    vm((32, B), I32), pltpu.SMEM((32, B), I32),
    vm((2 * FL, VD), BF16), vm((32, FL, B)), vm((32, FL, B)),
    vm((4, 4, 2, 32, B)), vm((4, 4, 2, 32, B)), vm((FL, B)),
    vm((32, 2 * FL, B), BF16), vm((32, 2 * FL, B), BF16), vm((LT, H, B)), vm((HT, FL, B)),
    vm((4, FL, CH)), vm((4, FL, CH)), vm((4, FL, CH)), vm((FL, B)), vm((4, FL, B)),
    vm((4, FL, CH), BF16), vm((4, FL, CH), BF16), vm((4, FL, 256), BF16), vm((4, FL, 256), BF16),
    vm((4, FL, 256), BF16), vm((4, FL, 256), BF16), vm((4, FL, CH), BF16), vm((4, FL, CH), BF16),
    vm((4, FL, CH)), vm((4, FL, CH)), vm((4, FL, CH)), vm((NB, 2 * FL, B), BF16),
    vm((32, FL, B)), vm((32, FL, B)), vm((4, 4, 2, FL, B)), vm((4, 4, FL, B)), vm((4, 4, FL, B)),
    vm((3, 4, 32, B)), vm((3, 4, 32, B)), vm((4, 32, B)), vm((4, 32, B)),
    vm((3, 32, B)), vm((3, 32, B)), vm((4, 72, 256)), vm((3, 72, 256)), vm((2, 72, B)),
    vm((72, B)), vm((72, B)), vm((3, 72, B)), vm((72, B)), vm((3, 72, B)), vm((2, 72, B)),
    vm((FL, VD)),
    pltpu.SemaphoreType.DMA((8,)), pltpu.SemaphoreType.DMA((NSEM,)),
    pltpu.SemaphoreType.DMA((NSEM,)),
]


def shards(
    features, weight, bias, cotangent, send_index, send_count, hub_local,
    low_tiles, low_src, low_dst, hub_tiles, hub_src, hub_dst,
):
    hbm = pl.BlockSpec(memory_space=pl.ANY)
    vmem = pl.BlockSpec(memory_space=pltpu.VMEM)
    results = pl.pallas_call(
        kernel,
        out_shape=(
            jax.ShapeDtypeStruct((FL, VD), F32),
            jax.ShapeDtypeStruct((FL, VD), F32),
            jax.ShapeDtypeStruct((FL, 256), F32),
            jax.ShapeDtypeStruct((1, FL), F32),
        ),
        in_specs=[hbm, hbm, vmem, hbm, vmem, vmem, vmem, hbm, hbm, vmem, vmem, vmem, vmem],
        out_specs=(hbm, hbm, vmem, vmem),
        scratch_shapes=SCRATCH,
        compiler_params=pltpu.CompilerParams(
            collective_id=0, has_side_effects=True, vmem_limit_bytes=60 * 2**20
        ),
        cost_estimate=pl.CostEstimate(
            flops=4 * 10**9, bytes_accessed=16 * 2**20, transcendentals=131072
        ),
    )(
        features, weight, bias[None, :], cotangent, send_index.reshape(32, B), send_count,
        hub_local[None, :], low_tiles, hub_tiles,
        low_src[None, :], low_dst[None, :], hub_src[None, :], hub_dst[None, :],
    )
    out, fg, wg, bg = pl.pallas_call(
        hand_over,
        out_shape=tuple(jax.ShapeDtypeStruct(r.shape, r.dtype) for r in results),
        in_specs=[hbm] * 4,
        out_specs=(hbm,) * 4,
        scratch_shapes=[
            vm((FL, VD)), vm((FL, VD)), vm((FL, 256)), vm((1, FL)),
            pltpu.SemaphoreType.DMA((6,)), pltpu.SemaphoreType.DMA((6,)),
        ],
        compiler_params=pltpu.CompilerParams(vmem_limit_bytes=60 * 2**20),
    )(*results)
    return out, fg, wg, bg[0]


def solution(mesh):
    return jax.shard_map(
        shards,
        mesh=mesh,
        in_specs=(
            P("rep", "dom"),
            P(),
            P("rep"),
            P("rep", "dom"),
            P("dom", None),
            P("dom", None),
            P("dom"),
            P("dom", None, None),
            P("dom"),
            P("dom"),
            P("dom", None, None),
            P("dom"),
            P("dom"),
        ),
        out_specs=(P("rep", "dom"), P("rep", "dom"), P("rep", None), P("rep")),
        check_vma=False,
    )
```

```python
import math

import jax
import jax.numpy as jnp
from jax import lax
from jax.experimental import pallas as pl
from jax.experimental.pallas import tpu as pltpu
from jax.sharding import PartitionSpec as P

F32 = jnp.float32
BF16 = jnp.bfloat16
I32 = jnp.int32
NN = (((1,), (0,)), ((), ()))
NT = (((1,), (1,)), ((), ()))
MESH = pl.DeviceIdType.MESH

FL = 64
VD = 2048
CH = 512
B = 128
LT, HT = 128, 64
NB = 16
UNROLL = 32

OFFSETS = sorted(
    [(i, j, k) for i in range(4) for j in range(4) for k in range(2) if (i, j, k) != (0, 0, 0)],
    key=lambda o: (-min(o[0], 4 - o[0]) - min(o[1], 4 - o[1]), o[2]),
)
CHIPS = [(i, j) for i, j, k in OFFSETS if k == 0]
CHIPS_X = sum(i << (2 * n) for n, (i, j) in enumerate(CHIPS))
CHIPS_Y = sum(j << (2 * n) for n, (i, j) in enumerate(CHIPS))
FIRST = 6
H = FL // 2

LOW, BACK = (0, 1, 2), ((3, 4, 5), (6, 7, 8))
COT, SUM, GRAD, OUT, WZ = 9, (10, 11), (12, 13), 14, 15
HUB1, HUB2, HUB3, RED0, RED1, RED2, WC, WX, WY, WC2 = range(16, 26)
NSEM = 26


def mm(a, b, dims):
    return lax.dot_general(a, b, dims, preferred_element_type=F32)


def split(x):
    high = x.astype(BF16)
    return high, (x - high.astype(F32)).astype(BF16)


def fold(r):
    return r[:FL] + r[FL:]


def place(idx):
    return (lax.broadcasted_iota(I32, (VD, idx.shape[1]), 0) == idx).astype(BF16)


def place_t(col):
    lanes = lax.broadcasted_iota(I32, (col.shape[0], VD), 1)
    return (lanes == jnp.concatenate([col] * (VD // B), axis=1)).astype(BF16)


def halves(r):
    parts = [r[i : i + H] + r[i + H : i + 2 * H] for i in range(0, r.shape[0], 2 * H)]
    return parts[0] if len(parts) == 1 else jnp.concatenate(parts, axis=0)


def split_into(ref, i, half, value):
    high, low = split(value)
    ref[i, 2 * H * half : 2 * H * half + H] = high
    ref[i, 2 * H * half + H : 2 * H * half + 2 * H] = low


def order(key, other):
    n = key.shape[1]
    lane = lax.broadcasted_iota(I32, (n, n), 1)
    sub = lax.broadcasted_iota(I32, (n, n), 0)
    eye = lane == sub
    key = jnp.broadcast_to(key, (n, n))
    other = jnp.broadcast_to(other, (n, n))
    key_col = jnp.sum(jnp.where(eye, key, 0), axis=1, keepdims=True)
    other_col = jnp.sum(jnp.where(eye, other, 0), axis=1, keepdims=True)
    less = jnp.sum(jnp.where(key < key_col, 1, 0), axis=1, keepdims=True)
    before = (key == key_col) & (lane < sub)
    rank = less + jnp.sum(jnp.where(before, 1, 0), axis=1, keepdims=True)
    hot = rank == lane
    perm = jnp.sum(jnp.where(hot, sub, 0), axis=0, keepdims=True)
    other_row = jnp.sum(jnp.where(hot, other_col, 0), axis=0, keepdims=True)
    keep = jnp.sum(jnp.where(hot & (rank != less), 1, 0), axis=0, keepdims=True)
    count = jnp.sum(jnp.where(key_col <= lane, 1, 0), axis=0, keepdims=True)
    has = jnp.sum(jnp.where(key_col == lane, 1, 0), axis=0, keepdims=True)
    return [perm, other_row, keep, jnp.maximum(count - 1, 0), has]


def kernel(
    feat_h, weight_h, bias_v, cot_h, index_v, count_v, hub_v, low_h, hubt_h, ls_v, ld_v, hs_v, hd_v,
    out_h, fg_h, wg_o, bg_o,
    idx_v, idx_c, hub_c, feat, weight, cot, tile_f, tile_b, tile_t, table_v, table, xs, sbuf, lowr,
    hub_a, hub_b, own_hub, x_low, x_hub, seg, hseg, zsum, sumf, cotf, biasb, biasf, s_hi, s_lo,
    w_hi, w_lo, t_hi, t_lo, p_hi, p_lo, outc, gsend, gradf, x_grad, bbuf, backr, hpart, hcore, hsum,
    r_a, r_b, t_a, t_b, q_a, q_b, wgs, wzr, w1, wcr, w2, wxr, w3, wyr, wfin, acc,
    lsem, ss, rs,
):
    me = lax.axis_index("dom")
    z = lax.axis_index("rep")
    x, y, c = me // 8, lax.rem(me // 2, 4), lax.rem(me, 2)

    def dev(px, py, pc):
        return (lax.rem(px, 4) * 4 + lax.rem(py, 4)) * 2 + pc

    def at_x(d):
        return {"dom": dev(x + d, y, c), "rep": z}

    def at_y(d):
        return {"dom": dev(x, y + d, c), "rep": z}

    def at_z(d):
        return {"dom": me, "rep": lax.rem(z + d, 4)}

    at_core = {"dom": dev(x, y, 1 - c), "rep": z}

    def remote(src, dst, sem, target):
        return pltpu.make_async_remote_copy(
            src_ref=src, dst_ref=dst, send_sem=ss.at[sem], recv_sem=rs.at[sem],
            device_id=target, device_id_type=MESH,
        )

    sent = {}

    def unit(n):
        return lowr.at[pl.ds(0, n), pl.ds(0, H)]

    def send(src, dst, sem, target):
        remote(src, dst, sem, target).start()
        sent.setdefault(sem, []).append(math.prod(src.shape))

    def size(sem):
        total = sum(sent[sem])
        if sem == WZ:
            return wzr
        if sem in (WX, WY):
            return wxr
        if sem in (WC, WC2):
            return wcr
        return unit(total // (H * B))

    def arrived(sem):
        remote(size(sem), size(sem), sem, at_core).wait_recv()

    loads = [
        pltpu.make_async_copy(s, d, lsem.at[i])
        for i, (s, d) in enumerate(
            [(feat_h, feat), (cot_h, cot), (weight_h, weight),
             (low_h, tile_f), (hubt_h, tile_f.at[pl.ds(0, HT)])]
        )
    ]
    for load in loads[:4]:
        load.start()

    barrier = pltpu.get_barrier_semaphore()

    def greet(i, _):
        other = lax.rem(me + i, 32)
        pl.semaphore_signal(barrier, inc=1, device_id={"dom": other, "rep": z}, device_id_type=MESH)
        return 0

    lax.fori_loop(1, 32, greet, 0)
    for d in (1, 2, 3):
        pl.semaphore_signal(barrier, inc=1, device_id=at_z(d), device_id_type=MESH)

    lane = lax.broadcasted_iota(I32, (32, B), 1)
    sub = lax.broadcasted_iota(I32, (32, 32), 0)
    eye = sub == lax.broadcasted_iota(I32, (32, 32), 1)
    count = jnp.broadcast_to(count_v[...], (32, 32))
    count = jnp.sum(jnp.where(eye, count, 0), axis=1, keepdims=True)
    idx_v[...] = jnp.where(lane < count, index_v[...], -1)
    eye = lax.broadcasted_iota(I32, (FL, FL), 0) == lax.broadcasted_iota(I32, (FL, FL), 1)
    bias = jnp.where(eye, jnp.broadcast_to(bias_v[...], (FL, FL)), 0.0)
    biasb[...] = jnp.broadcast_to(jnp.sum(bias, axis=1, keepdims=True), (FL, B))

    loads[0].wait()
    high, low = split(feat[...])
    xs[0:FL] = high
    xs[FL:] = low
    own_hub[...] = fold(mm(xs[...], place(hub_v[...]), NN))
    hub_a[x, y, c] = own_hub[0:32]
    hub_b[x, y, c] = own_hub[32:64]

    def gather_pair(i, _):
        idx = jnp.concatenate([idx_v[pl.ds(2 * i, 1), :], idx_v[pl.ds(2 * i + 1, 1), :]], axis=1)
        rows = fold(mm(xs[...], place(idx), NN))
        sbuf[2 * i] = rows[:, :B]
        sbuf[2 * i + 1] = rows[:, B:]
        return 0

    lax.fori_loop(0, 16, gather_pair, 0)
    lowr[me] = sbuf[me]
    pl.semaphore_wait(barrier, 34)

    for d in (2, 1, 3):
        send(hub_a.at[x, y, c], hub_a.at[x, y, c], HUB1, at_x(d))
        send(hub_b.at[x, y, c], hub_b.at[x, y, c], HUB1, at_y(d))

    def rows_of(half):
        return pl.ds(half * H, H)

    def exchange(src, dst, half, group, begin=0, end=31):
        part = rows_of(half)
        for dx, dy, dc in OFFSETS[begin:end]:
            to = dev(x + dx, y + dy, lax.rem(c + dc, 2))
            sem = group(dx, dy)
            send(src.at[to, part], dst.at[me, part], sem, {"dom": to, "rep": z})

    def chip(j):
        return (CHIPS_X >> (2 * j)) & 3, (CHIPS_Y >> (2 * j)) & 3

    exchange(sbuf, lowr, 0, lambda dx, dy: LOW[0], 0, FIRST)

    arrived(HUB1)
    for d in (2, 1, 3):
        send(hub_a.at[:, y, c], hub_a.at[:, y, c], HUB2, at_y(d))
        send(hub_b.at[x, :, c], hub_b.at[x, :, c], HUB2, at_x(d))

    exchange(sbuf, lowr, 0, lambda dx, dy: LOW[1], FIRST, 31)

    loads[1].wait()
    for d in (2, 1, 3):
        other = lax.rem(z + d, 4)
        chunk = pl.ds(pl.multiple_of(other * CH, CH), CH)
        send(cot.at[:, chunk], cotf.at[z], COT, at_z(d))
        send(biasb, biasf.at[z], COT, at_z(d))
    cotf[z] = cot[:, pl.ds(pl.multiple_of(z * CH, CH), CH)]
    biasf[z] = biasb[...]

    keys = [(ld_v, ls_v), (hd_v, hs_v), (ls_v, ld_v), (hs_v, hd_v)]
    for i, (a, b) in enumerate(keys):
        for r, row in enumerate(order(a[...], b[...])):
            table_v[i * 8 + r : i * 8 + r + 1, 0 : row.shape[1]] = row
    to_scalars = pltpu.make_async_copy(table_v, table, lsem.at[5])
    to_scalars.start()

    loads[2].wait()
    w = weight[...]
    wt = jnp.transpose(w)
    high, low = split(w)
    w_hi[...] = high.reshape(4, FL, 256)
    w_lo[...] = low.reshape(4, FL, 256)
    high, low = split(wt)
    t_hi[...] = high.reshape(4, FL, 256)
    t_lo[...] = low.reshape(4, FL, 256)

    square = lax.broadcasted_iota(I32, (B, B), 0) == lax.broadcasted_iota(I32, (B, B), 1)

    def column(row):
        picked = jnp.where(square, jnp.broadcast_to(row, (B, B)), 0)
        return jnp.broadcast_to(jnp.sum(picked, axis=1, keepdims=True), (B, B))

    def columns(i, _):
        idx_c[i] = column(idx_v[pl.ds(i, 1), :])
        return 0

    lax.fori_loop(0, 32, columns, 0)
    hub_c[...] = column(hub_v[...])

    def convert(base):
        def step(g, _):
            for u in range(4):
                t = g * 4 + u
                tile = tile_f[t]
                h, l = split(tile)
                tile_b[base + t, :, 0:B] = h
                tile_b[base + t, :, B:] = l
                h, l = split(jnp.transpose(tile))
                tile_t[base + t, :, 0:B] = h
                tile_t[base + t, :, B:] = l
            return 0

        return step

    arrived(LOW[0])
    exchange(sbuf, lowr, 1, lambda dx, dy: LOW[2])
    loads[3].wait()
    lax.fori_loop(0, HT // 4, convert(0), 0)
    loads[4].start()
    lax.fori_loop(HT // 4, LT // 4, convert(0), 0)
    to_scalars.wait()

    arrived(HUB2)
    send(hub_a.at[:, :, c], hub_a.at[:, :, c], HUB3, at_core)
    send(hub_b.at[:, :, c], hub_b.at[:, :, c], HUB3, at_core)
    loads[4].wait()
    lax.fori_loop(0, HT // 4, convert(LT), 0)

    def tiles(which, count, base, source, values, out):
        row = which * 8
        last_source = (NB if which >= 2 else 32) - 1

        def step(g, total):
            parts = []
            for u in range(UNROLL):
                t = g * UNROLL + u
                p = jnp.clip(table[row, t], 0, count - 1)
                s = jnp.clip(table[row + 1, t], 0, last_source)
                r = halves(mm(source(s), values[base + p], NN))
                parts.append(r[:, :B] + r[:, B:])
            for u in range(UNROLL):
                t = g * UNROLL + u
                total = parts[u] + jnp.where(table[row + 2, t] == 0, 0.0, total)
                out[t] = total
            return total

        lax.fori_loop(0, count // UNROLL, step, jnp.zeros(out.shape[1:], F32))

    def block(which, ref, b):
        found = ref[jnp.clip(table[which * 8 + 3, b], 0, ref.shape[0] - 1)]
        return jnp.where(table[which * 8 + 4, b] == 0, 0.0, found)

    def half_of(ref, half):
        return lambda s: ref[s, 2 * H * half : 2 * H * (half + 1)]

    def take_low(half):
        for sem in (LOW[2:], LOW[1:2])[half == 0]:
            arrived(sem)

        def split_low(g, _):
            for u in range(4):
                split_into(x_low, g * 4 + u, half, lowr[g * 4 + u, half * H : half * H + H])
            return 0

        lax.fori_loop(0, 8, split_low, 0)
        tiles(0, LT, 0, half_of(x_low, half), tile_t, seg)

    def split_hub(g, _):
        for u in range(4):
            i = g * 4 + u
            ix, iy, ic = i // 8, lax.rem(i // 2, 4), lax.rem(i, 2)
            split_into(x_hub, i, 0, hub_a[ix, iy, ic])
            split_into(x_hub, i, 1, hub_b[ix, iy, ic])
        return 0

    def sums(half):
        part = rows_of(half)

        def value(b):
            hub = jnp.where(table[12, b] == 0, 0.0, hseg[jnp.clip(table[11, b], 0, HT - 1), part])
            return block(0, seg, b) + hub

        for d in (2, 1, 3):
            for i in range(4):
                zsum[d, part, i * B : (i + 1) * B] = value(lax.rem(z + d, 4) * 4 + i)
            send(zsum.at[d, part], sumf.at[z, part], SUM[half], at_z(d))
        for i in range(4):
            sumf[z, part, i * B : (i + 1) * B] = value(z * 4 + i)

    arrived(HUB3)
    lax.fori_loop(0, 8, split_hub, 0)
    tiles(1, HT, LT, lambda s: x_hub[s], tile_t, hseg)
    take_low(0)
    sums(0)
    take_low(1)
    sums(1)
    for sem in (COT, SUM[0], SUM[1]):
        arrived(sem)

    high, low = split(sumf[...])
    s_hi[...] = high
    s_lo[...] = low

    def dense(zc, _):
        r = fold(mm(jnp.concatenate([t_hi[zc], t_lo[zc]], axis=0), s_hi[...].reshape(256, CH), NN))
        r = r + mm(t_hi[zc], s_lo[...].reshape(256, CH), NN)
        bias = biasf[zc]
        pre = r + jnp.concatenate([bias] * 4, axis=1)
        sig = jax.nn.sigmoid(pre)
        outc[zc] = pre * sig
        grad = cotf[zc] * sig * (1.0 + pre * (1.0 - sig))
        h, l = split(grad)
        p_hi[zc] = h
        p_lo[zc] = l
        return 0

    lax.fori_loop(0, 4, dense, 0)

    def back_rows(zc):
        both = jnp.concatenate([w_hi[zc], w_lo[zc]], axis=0)
        r = fold(mm(both, p_hi[...].reshape(256, CH), NN))
        return r + mm(w_hi[zc], p_lo[...].reshape(256, CH), NN)

    def send_grad(half, d):
        part = rows_of(half)
        send(gsend.at[d, part], gradf.at[z, part], GRAD[half], at_z(d))

    for d in (2, 1, 3):
        gsend[d] = back_rows(lax.rem(z + d, 4))
        send_grad(0, d)
    for d in (2, 1, 3):
        send_grad(1, d)
    gradf[z] = back_rows(z)

    def out_part():
        return out_h.at[:, pl.ds(pl.multiple_of(z * CH, CH), CH)]

    def weight_rows(zc, _):
        both = jnp.concatenate([s_hi[zc], s_lo[zc]], axis=0)
        r = fold(mm(both, p_hi[...].reshape(256, CH), NT))
        r = r + mm(s_hi[zc], p_lo[...].reshape(256, CH), NT)
        ones = jnp.ones((16, CH), BF16)
        bsum = mm(ones, p_hi[...].reshape(256, CH), NT) + mm(ones, p_lo[...].reshape(256, CH), NT)
        wgs[zc, 0:FL] = r
        wgs[zc, FL:] = bsum[0:8]
        return 0

    lax.fori_loop(0, 4, weight_rows, 0)
    for d in (2, 1, 3):
        send(wgs.at[lax.rem(z + d, 4)], wzr.at[d - 1], WZ, at_z(d))

    for d in (2, 1, 3):
        send(outc.at[lax.rem(z + d, 4)], out_part(), OUT, at_z(d))
    own_out = pltpu.make_async_copy(outc.at[z], out_part(), lsem.at[6])
    own_out.start()


    def take_grad(half):
        arrived(GRAD[half])
        for b in range(NB):
            value = gradf[b // 4, half * H : half * H + H, (b % 4) * B : (b % 4 + 1) * B]
            split_into(x_grad, b, half, value)

    def low_blocks(half):
        tiles(2, LT, 0, half_of(x_grad, half), tile_b, seg)

        def put(g, _):
            for u in range(4):
                bbuf[g * 4 + u, half * H : half * H + H] = block(2, seg, g * 4 + u)
            return 0

        lax.fori_loop(0, 8, put, 0)
        backr[me, half * H : half * H + H] = bbuf[me, half * H : half * H + H]

    take_grad(0)
    low_blocks(0)

    def back_group(half):
        return lambda dx, dy: BACK[half][CHIPS.index((dx, dy)) // 5 if dx + dy > 0 else 2]

    exchange(bbuf, backr, 0, back_group(0))

    take_grad(1)
    low_blocks(1)
    exchange(bbuf, backr, 1, back_group(1))

    tiles(3, HT, LT, lambda s: x_grad[s], tile_b, hseg)

    def hub_blocks(g, _):
        for u in range(4):
            i = g * 4 + u
            hpart[i // 8, lax.rem(i // 2, 4), lax.rem(i, 2)] = block(3, hseg, i)
        return 0

    lax.fori_loop(0, 8, hub_blocks, 0)
    send(hpart.at[:, :, 1 - c], hcore, RED0, at_core)

    arrived(RED0)
    hsum[...] = hpart[:, :, c] + hcore[...]
    for d in (2, 1, 3):
        src = hsum.at[lax.rem(x + d, 4), :, pl.ds(0, 32)]
        send(src, r_a.at[d - 1], RED1, at_x(d))
        src = hsum.at[:, lax.rem(y + d, 4), pl.ds(32, 32)]
        send(src, r_b.at[d - 1], RED1, at_y(d))

    acc[...] = jnp.zeros((FL, VD), F32)

    def add_pair(half, first):
        part = slice(half * H, half * H + H)
        h, l = split(jnp.concatenate([backr[first, part], backr[first + 1, part]], axis=1))
        col = jnp.concatenate([idx_c[first], idx_c[first + 1]], axis=0)
        acc[part, :] += halves(mm(jnp.concatenate([h, l], axis=0), place_t(col), NN))

    def take_back(half, group):
        def step(j, _):
            dx, dy = chip(j)
            add_pair(half, dev(x + 4 - dx, y + 4 - dy, 0))
            return 0

        arrived(BACK[half][group])
        lax.fori_loop(group * 5, group * 5 + 5, step, 0)
        if group == 2:
            add_pair(half, dev(x, y, 0))

    take_back(0, 0)
    arrived(WZ)
    total = wgs[z] + wzr[0] + wzr[1] + wzr[2]
    w1[0] = total[:, :B]
    w1[1] = total[:, B:]
    send(w1.at[1 - c], wcr, WC, at_core)
    take_back(0, 1)
    arrived(WC)
    w2[...] = w1[c] + wcr[...]
    for d in (2, 1, 3):
        send(w2, wxr.at[d - 1], WX, at_x(d))
    take_back(0, 2)

    arrived(RED1)
    t_a[...] = hsum[x, :, 0:32] + r_a[0] + r_a[1] + r_a[2]
    t_b[...] = hsum[:, y, 32:64] + r_b[0] + r_b[1] + r_b[2]
    for d in (2, 1, 3):
        send(t_a.at[lax.rem(y + d, 4)], q_a.at[d - 1], RED2, at_y(d))
        send(t_b.at[lax.rem(x + d, 4)], q_b.at[d - 1], RED2, at_x(d))

    arrived(WX)
    w3[...] = w2[...] + wxr[0] + wxr[1] + wxr[2]
    for d in (2, 1, 3):
        send(w3, wyr.at[d - 1], WY, at_y(d))
    take_back(1, 0)
    take_back(1, 1)
    arrived(WY)
    wfin[c] = w3[...] + wyr[0] + wyr[1] + wyr[2]
    send(wfin.at[c], wfin.at[c], WC2, at_core)
    take_back(1, 2)

    arrived(RED2)
    h_a, l_a = split(t_a[y] + q_a[0] + q_a[1] + q_a[2])
    h_b, l_b = split(t_b[x] + q_b[0] + q_b[1] + q_b[2])
    both = jnp.concatenate([h_a, h_b, l_a, l_b], axis=0)
    acc[...] += fold(mm(both, place_t(hub_c[...]), NN))
    store = pltpu.make_async_copy(acc, fg_h, lsem.at[7])
    store.start()

    arrived(WC2)
    scale = 1.0 / math.sqrt(VD * 32)
    wg_o[:, :B] = wfin[0, 0:FL] * scale
    wg_o[:, B:] = wfin[1, 0:FL] * scale
    row = jnp.concatenate([wfin[0, FL : FL + 1], wfin[1, FL : FL + 1]], axis=1)
    mine = jnp.zeros((1, FL), F32)
    for i in range(4):
        mine = mine + jnp.where(z == i, row[:, i * FL : (i + 1) * FL], 0.0)
    bg_o[...] = mine * scale

    arrived(OUT)
    own_out.wait()
    store.wait()

    for sem in sent:
        remote(size(sem), size(sem), sem, at_core).wait_send()


def hand_over(a, b, c, d, out_a, out_b, out_c, out_d, va, vb, vc, vd, sem_in, sem_out):
    rows = [pl.ds(0, 32), pl.ds(32, 32)]
    trips = [(r.at[h], v.at[h], o.at[h]) for h in rows for r, v, o in [(a, va, out_a), (b, vb, out_b)]]
    trips += [(c, vc, out_c), (d, vd, out_d)]
    fetch = [pltpu.make_async_copy(r, v, sem_in.at[i]) for i, (r, v, _) in enumerate(trips)]
    store = [pltpu.make_async_copy(v, o, sem_out.at[i]) for i, (_, v, o) in enumerate(trips)]
    for copy in fetch:
        copy.start()
    for first, then in zip(fetch, store):
        first.wait()
        then.start()
    for copy in store:
        copy.wait()


def vm(shape, dtype=F32):
    return pltpu.VMEM(shape, dtype)


SCRATCH = [
    vm((32, B), I32), vm((32, B, B), I32), vm((B, B), I32),
    vm((FL, VD)), vm((256, 256)), vm((FL, VD)), vm((LT, B, B)),
    vm((LT + HT, B, 2 * B), BF16), vm((LT + HT, B, 2 * B), BF16),
    vm((32, B), I32), pltpu.SMEM((32, B), I32),
    vm((2 * FL, VD), BF16), vm((32, FL, B)), vm((32, FL, B)),
    vm((4, 4, 2, 32, B)), vm((4, 4, 2, 32, B)), vm((FL, B)),
    vm((32, 2 * FL, B), BF16), vm((32, 2 * FL, B), BF16), vm((LT, H, B)), vm((HT, FL, B)),
    vm((4, FL, CH)), vm((4, FL, CH)), vm((4, FL, CH)), vm((FL, B)), vm((4, FL, B)),
    vm((4, FL, CH), BF16), vm((4, FL, CH), BF16), vm((4, FL, 256), BF16), vm((4, FL, 256), BF16),
    vm((4, FL, 256), BF16), vm((4, FL, 256), BF16), vm((4, FL, CH), BF16), vm((4, FL, CH), BF16),
    vm((4, FL, CH)), vm((4, FL, CH)), vm((4, FL, CH)), vm((NB, 2 * FL, B), BF16),
    vm((32, FL, B)), vm((32, FL, B)), vm((4, 4, 2, FL, B)), vm((4, 4, FL, B)), vm((4, 4, FL, B)),
    vm((3, 4, 32, B)), vm((3, 4, 32, B)), vm((4, 32, B)), vm((4, 32, B)),
    vm((3, 32, B)), vm((3, 32, B)), vm((4, 72, 256)), vm((3, 72, 256)), vm((2, 72, B)),
    vm((72, B)), vm((72, B)), vm((3, 72, B)), vm((72, B)), vm((3, 72, B)), vm((2, 72, B)),
    vm((FL, VD)),
    pltpu.SemaphoreType.DMA((8,)), pltpu.SemaphoreType.DMA((NSEM,)),
    pltpu.SemaphoreType.DMA((NSEM,)),
]


def shards(
    features, weight, bias, cotangent, send_index, send_count, hub_local,
    low_tiles, low_src, low_dst, hub_tiles, hub_src, hub_dst,
):
    hbm = pl.BlockSpec(memory_space=pl.ANY)
    vmem = pl.BlockSpec(memory_space=pltpu.VMEM)
    results = pl.pallas_call(
        kernel,
        out_shape=(
            jax.ShapeDtypeStruct((FL, VD), F32),
            jax.ShapeDtypeStruct((FL, VD), F32),
            jax.ShapeDtypeStruct((FL, 256), F32),
            jax.ShapeDtypeStruct((1, FL), F32),
        ),
        in_specs=[hbm, hbm, vmem, hbm, vmem, vmem, vmem, hbm, hbm, vmem, vmem, vmem, vmem],
        out_specs=(hbm, hbm, vmem, vmem),
        scratch_shapes=SCRATCH,
        compiler_params=pltpu.CompilerParams(
            collective_id=0, has_side_effects=True, vmem_limit_bytes=60 * 2**20
        ),
        cost_estimate=pl.CostEstimate(
            flops=4 * 10**9, bytes_accessed=16 * 2**20, transcendentals=131072
        ),
    )(
        features, weight, bias[None, :], cotangent, send_index.reshape(32, B), send_count,
        hub_local[None, :], low_tiles, hub_tiles,
        low_src[None, :], low_dst[None, :], hub_src[None, :], hub_dst[None, :],
    )
    out, fg, wg, bg = pl.pallas_call(
        hand_over,
        out_shape=tuple(jax.ShapeDtypeStruct(r.shape, r.dtype) for r in results),
        in_specs=[hbm] * 4,
        out_specs=(hbm,) * 4,
        scratch_shapes=[
            vm((FL, VD)), vm((FL, VD)), vm((FL, 256)), vm((1, FL)),
            pltpu.SemaphoreType.DMA((6,)), pltpu.SemaphoreType.DMA((6,)),
        ],
        compiler_params=pltpu.CompilerParams(vmem_limit_bytes=60 * 2**20),
    )(*results)
    return out, fg, wg, bg[0]


def solution(mesh):
    return jax.shard_map(
        shards,
        mesh=mesh,
        in_specs=(
            P("rep", "dom"),
            P(),
            P("rep"),
            P("rep", "dom"),
            P("dom", None),
            P("dom", None),
            P("dom"),
            P("dom", None, None),
            P("dom"),
            P("dom"),
            P("dom", None, None),
            P("dom"),
            P("dom"),
        ),
        out_specs=(P("rep", "dom"), P("rep", "dom"), P("rep", None), P("rep")),
        check_vma=False,
    )
```

```python
import math

import jax
import jax.numpy as jnp
from jax import lax
from jax.experimental import pallas as pl
from jax.experimental.pallas import tpu as pltpu
from jax.sharding import PartitionSpec as P

F32 = jnp.float32
BF16 = jnp.bfloat16
I32 = jnp.int32
NN = (((1,), (0,)), ((), ()))
NT = (((1,), (1,)), ((), ()))
MESH = pl.DeviceIdType.MESH

FL = 64
VD = 2048
CH = 512
B = 128
LT, HT = 128, 64
NB = 16
UNROLL = 32

OFFSETS = sorted(
    [(i, j, k) for i in range(4) for j in range(4) for k in range(2) if (i, j, k) != (0, 0, 0)],
    key=lambda o: (-min(o[0], 4 - o[0]) - min(o[1], 4 - o[1]), o[2]),
)
CHIPS = [(i, j) for i, j, k in OFFSETS if k == 0]
CHIPS_X = sum(i << (2 * n) for n, (i, j) in enumerate(CHIPS))
CHIPS_Y = sum(j << (2 * n) for n, (i, j) in enumerate(CHIPS))
FIRST = 6
H = FL // 2

LOW, BACK = (0, 1, 2), ((3, 4, 5), (6, 7, 8))
COT, SUM, GRAD, OUT, WZ = 9, (10, 11), (12, 13), 14, 15
HUB1, HUB2, HUB3, RED0, RED1, RED2, WC, WX, WY, WC2 = range(16, 26)
NSEM = 26


def mm(a, b, dims):
    return lax.dot_general(a, b, dims, preferred_element_type=F32)


def split(x):
    high = x.astype(BF16)
    return high, (x - high.astype(F32)).astype(BF16)


def fold(r):
    return r[:FL] + r[FL:]


def place(idx):
    return (lax.broadcasted_iota(I32, (VD, idx.shape[1]), 0) == idx).astype(BF16)


def place_t(col):
    lanes = lax.broadcasted_iota(I32, (col.shape[0], VD), 1)
    return (lanes == jnp.concatenate([col] * (VD // B), axis=1)).astype(BF16)


def halves(r):
    parts = [r[i : i + H] + r[i + H : i + 2 * H] for i in range(0, r.shape[0], 2 * H)]
    return parts[0] if len(parts) == 1 else jnp.concatenate(parts, axis=0)


def split_into(ref, i, half, value):
    high, low = split(value)
    ref[i, 2 * H * half : 2 * H * half + H] = high
    ref[i, 2 * H * half + H : 2 * H * half + 2 * H] = low


def order(key, other):
    n = key.shape[1]
    lane = lax.broadcasted_iota(I32, (n, n), 1)
    sub = lax.broadcasted_iota(I32, (n, n), 0)
    eye = lane == sub
    key = jnp.broadcast_to(key, (n, n))
    other = jnp.broadcast_to(other, (n, n))
    key_col = jnp.sum(jnp.where(eye, key, 0), axis=1, keepdims=True)
    other_col = jnp.sum(jnp.where(eye, other, 0), axis=1, keepdims=True)
    less = jnp.sum(jnp.where(key < key_col, 1, 0), axis=1, keepdims=True)
    before = (key == key_col) & (lane < sub)
    rank = less + jnp.sum(jnp.where(before, 1, 0), axis=1, keepdims=True)
    hot = rank == lane
    perm = jnp.sum(jnp.where(hot, sub, 0), axis=0, keepdims=True)
    other_row = jnp.sum(jnp.where(hot, other_col, 0), axis=0, keepdims=True)
    keep = jnp.sum(jnp.where(hot & (rank != less), 1, 0), axis=0, keepdims=True)
    count = jnp.sum(jnp.where(key_col <= lane, 1, 0), axis=0, keepdims=True)
    has = jnp.sum(jnp.where(key_col == lane, 1, 0), axis=0, keepdims=True)
    return [perm, other_row, keep, jnp.maximum(count - 1, 0), has]


def kernel(
    feat_h, weight_h, bias_v, cot_h, index_v, count_v, hub_v, low_h, hubt_h, ls_v, ld_v, hs_v, hd_v,
    out_h, fg_h, wg_o, bg_o,
    idx_v, idx_c, hub_c, feat, weight, cot, tile_f, tile_b, tile_t, table_v, table, xs, sbuf, lowr,
    hub_a, hub_b, own_hub, x_low, x_hub, seg, hseg, zsum, sumf, cotf, biasb, biasf, s_hi, s_lo,
    w_hi, w_lo, t_hi, t_lo, p_hi, p_lo, outc, gsend, gradf, x_grad, bbuf, backr, hpart, hcore, hsum,
    r_a, r_b, t_a, t_b, q_a, q_b, wgs, wzr, w1, wcr, w2, wxr, w3, wyr, wfin, acc,
    lsem, ss, rs,
):
    me = lax.axis_index("dom")
    z = lax.axis_index("rep")
    x, y, c = me // 8, lax.rem(me // 2, 4), lax.rem(me, 2)

    def dev(px, py, pc):
        return (lax.rem(px, 4) * 4 + lax.rem(py, 4)) * 2 + pc

    def at_x(d):
        return {"dom": dev(x + d, y, c), "rep": z}

    def at_y(d):
        return {"dom": dev(x, y + d, c), "rep": z}

    def at_z(d):
        return {"dom": me, "rep": lax.rem(z + d, 4)}

    at_core = {"dom": dev(x, y, 1 - c), "rep": z}

    def remote(src, dst, sem, target):
        return pltpu.make_async_remote_copy(
            src_ref=src, dst_ref=dst, send_sem=ss.at[sem], recv_sem=rs.at[sem],
            device_id=target, device_id_type=MESH,
        )

    sent = {}

    def unit(n):
        return lowr.at[pl.ds(0, n), pl.ds(0, H)]

    def send(src, dst, sem, target):
        remote(src, dst, sem, target).start()
        sent.setdefault(sem, []).append(math.prod(src.shape))

    def size(sem):
        total = sum(sent[sem])
        if sem == WZ:
            return wzr
        if sem in (WX, WY):
            return wxr
        if sem in (WC, WC2):
            return wcr
        return unit(total // (H * B))

    def arrived(sem):
        remote(size(sem), size(sem), sem, at_core).wait_recv()

    loads = [
        pltpu.make_async_copy(s, d, lsem.at[i])
        for i, (s, d) in enumerate(
            [(feat_h, feat), (cot_h, cot), (weight_h, weight),
             (low_h, tile_f), (hubt_h, tile_f.at[pl.ds(0, HT)])]
        )
    ]
    for load in loads[:4]:
        load.start()

    barrier = pltpu.get_barrier_semaphore()

    def greet(i, _):
        other = lax.rem(me + i, 32)
        pl.semaphore_signal(barrier, inc=1, device_id={"dom": other, "rep": z}, device_id_type=MESH)
        return 0

    lax.fori_loop(1, 32, greet, 0)
    for d in (1, 2, 3):
        pl.semaphore_signal(barrier, inc=1, device_id=at_z(d), device_id_type=MESH)

    lane = lax.broadcasted_iota(I32, (32, B), 1)
    sub = lax.broadcasted_iota(I32, (32, 32), 0)
    eye = sub == lax.broadcasted_iota(I32, (32, 32), 1)
    count = jnp.broadcast_to(count_v[...], (32, 32))
    count = jnp.sum(jnp.where(eye, count, 0), axis=1, keepdims=True)
    idx_v[...] = jnp.where(lane < count, index_v[...], -1)
    eye = lax.broadcasted_iota(I32, (FL, FL), 0) == lax.broadcasted_iota(I32, (FL, FL), 1)
    bias = jnp.where(eye, jnp.broadcast_to(bias_v[...], (FL, FL)), 0.0)
    biasb[...] = jnp.broadcast_to(jnp.sum(bias, axis=1, keepdims=True), (FL, B))

    loads[0].wait()
    high, low = split(feat[...])
    xs[0:FL] = high
    xs[FL:] = low
    own_hub[...] = fold(mm(xs[...], place(hub_v[...]), NN))
    hub_a[x, y, c] = own_hub[0:32]
    hub_b[x, y, c] = own_hub[32:64]

    def gather_pair(i, _):
        idx = jnp.concatenate([idx_v[pl.ds(2 * i, 1), :], idx_v[pl.ds(2 * i + 1, 1), :]], axis=1)
        rows = fold(mm(xs[...], place(idx), NN))
        sbuf[2 * i] = rows[:, :B]
        sbuf[2 * i + 1] = rows[:, B:]
        return 0

    lax.fori_loop(0, 16, gather_pair, 0)
    lowr[me] = sbuf[me]
    pl.semaphore_wait(barrier, 34)

    for d in (2, 1, 3):
        send(hub_a.at[x, y, c], hub_a.at[x, y, c], HUB1, at_x(d))
        send(hub_b.at[x, y, c], hub_b.at[x, y, c], HUB1, at_y(d))

    def rows_of(half):
        return pl.ds(half * H, H)

    def exchange(src, dst, half, group, begin=0, end=31):
        part = rows_of(half)
        for dx, dy, dc in OFFSETS[begin:end]:
            to = dev(x + dx, y + dy, lax.rem(c + dc, 2))
            sem = group(dx, dy)
            send(src.at[to, part], dst.at[me, part], sem, {"dom": to, "rep": z})

    def chip(j):
        return (CHIPS_X >> (2 * j)) & 3, (CHIPS_Y >> (2 * j)) & 3

    exchange(sbuf, lowr, 0, lambda dx, dy: LOW[0], 0, FIRST)

    arrived(HUB1)
    for d in (2, 1, 3):
        send(hub_a.at[:, y, c], hub_a.at[:, y, c], HUB2, at_y(d))
        send(hub_b.at[x, :, c], hub_b.at[x, :, c], HUB2, at_x(d))

    exchange(sbuf, lowr, 0, lambda dx, dy: LOW[1], FIRST, 31)

    loads[1].wait()
    for d in (2, 1, 3):
        other = lax.rem(z + d, 4)
        chunk = pl.ds(pl.multiple_of(other * CH, CH), CH)
        send(cot.at[:, chunk], cotf.at[z], COT, at_z(d))
        send(biasb, biasf.at[z], COT, at_z(d))
    cotf[z] = cot[:, pl.ds(pl.multiple_of(z * CH, CH), CH)]
    biasf[z] = biasb[...]

    keys = [(ld_v, ls_v), (hd_v, hs_v), (ls_v, ld_v), (hs_v, hd_v)]
    for i, (a, b) in enumerate(keys):
        for r, row in enumerate(order(a[...], b[...])):
            table_v[i * 8 + r : i * 8 + r + 1, 0 : row.shape[1]] = row
    to_scalars = pltpu.make_async_copy(table_v, table, lsem.at[5])
    to_scalars.start()

    loads[2].wait()
    w = weight[...]
    wt = jnp.transpose(w)
    high, low = split(w)
    w_hi[...] = high.reshape(4, FL, 256)
    w_lo[...] = low.reshape(4, FL, 256)
    high, low = split(wt)
    t_hi[...] = high.reshape(4, FL, 256)
    t_lo[...] = low.reshape(4, FL, 256)

    square = lax.broadcasted_iota(I32, (B, B), 0) == lax.broadcasted_iota(I32, (B, B), 1)

    def column(row):
        picked = jnp.where(square, jnp.broadcast_to(row, (B, B)), 0)
        return jnp.broadcast_to(jnp.sum(picked, axis=1, keepdims=True), (B, B))

    def columns(i, _):
        idx_c[i] = column(idx_v[pl.ds(i, 1), :])
        return 0

    lax.fori_loop(0, 32, columns, 0)
    hub_c[...] = column(hub_v[...])

    def convert(base):
        def step(g, _):
            for u in range(4):
                t = g * 4 + u
                tile = tile_f[t]
                h, l = split(tile)
                tile_b[base + t, :, 0:B] = h
                tile_b[base + t, :, B:] = l
                h, l = split(jnp.transpose(tile))
                tile_t[base + t, :, 0:B] = h
                tile_t[base + t, :, B:] = l
            return 0

        return step

    arrived(LOW[0])
    exchange(sbuf, lowr, 1, lambda dx, dy: LOW[2])

    arrived(HUB2)
    send(hub_a.at[:, :, c], hub_a.at[:, :, c], HUB3, at_core)
    send(hub_b.at[:, :, c], hub_b.at[:, :, c], HUB3, at_core)
    loads[3].wait()
    lax.fori_loop(0, HT // 4, convert(0), 0)
    loads[4].start()
    lax.fori_loop(HT // 4, LT // 4, convert(0), 0)
    to_scalars.wait()

    loads[4].wait()
    lax.fori_loop(0, HT // 4, convert(LT), 0)

    def tiles(which, count, base, source, values, out):
        row = which * 8
        last_source = (NB if which >= 2 else 32) - 1

        def step(g, total):
            parts = []
            for u in range(UNROLL):
                t = g * UNROLL + u
                p = jnp.clip(table[row, t], 0, count - 1)
                s = jnp.clip(table[row + 1, t], 0, last_source)
                r = halves(mm(source(s), values[base + p], NN))
                parts.append(r[:, :B] + r[:, B:])
            for u in range(UNROLL):
                t = g * UNROLL + u
                total = parts[u] + jnp.where(table[row + 2, t] == 0, 0.0, total)
                out[t] = total
            return total

        lax.fori_loop(0, count // UNROLL, step, jnp.zeros(out.shape[1:], F32))

    def block(which, ref, b):
        found = ref[jnp.clip(table[which * 8 + 3, b], 0, ref.shape[0] - 1)]
        return jnp.where(table[which * 8 + 4, b] == 0, 0.0, found)

    def half_of(ref, half):
        return lambda s: ref[s, 2 * H * half : 2 * H * (half + 1)]

    def take_low(half):
        for sem in (LOW[2:], LOW[1:2])[half == 0]:
            arrived(sem)

        def split_low(g, _):
            for u in range(4):
                split_into(x_low, g * 4 + u, half, lowr[g * 4 + u, half * H : half * H + H])
            return 0

        lax.fori_loop(0, 8, split_low, 0)
        tiles(0, LT, 0, half_of(x_low, half), tile_t, seg)

    def split_hub(g, _):
        for u in range(4):
            i = g * 4 + u
            ix, iy, ic = i // 8, lax.rem(i // 2, 4), lax.rem(i, 2)
            split_into(x_hub, i, 0, hub_a[ix, iy, ic])
            split_into(x_hub, i, 1, hub_b[ix, iy, ic])
        return 0

    def sums(half):
        part = rows_of(half)

        def value(b):
            hub = jnp.where(table[12, b] == 0, 0.0, hseg[jnp.clip(table[11, b], 0, HT - 1), part])
            return block(0, seg, b) + hub

        for d in (2, 1, 3):
            for i in range(4):
                zsum[d, part, i * B : (i + 1) * B] = value(lax.rem(z + d, 4) * 4 + i)
            send(zsum.at[d, part], sumf.at[z, part], SUM[half], at_z(d))
        for i in range(4):
            sumf[z, part, i * B : (i + 1) * B] = value(z * 4 + i)

    arrived(HUB3)
    lax.fori_loop(0, 8, split_hub, 0)
    tiles(1, HT, LT, lambda s: x_hub[s], tile_t, hseg)
    take_low(0)
    sums(0)
    take_low(1)
    sums(1)
    for sem in (COT, SUM[0], SUM[1]):
        arrived(sem)

    high, low = split(sumf[...])
    s_hi[...] = high
    s_lo[...] = low

    def dense(zc, _):
        r = fold(mm(jnp.concatenate([t_hi[zc], t_lo[zc]], axis=0), s_hi[...].reshape(256, CH), NN))
        r = r + mm(t_hi[zc], s_lo[...].reshape(256, CH), NN)
        bias = biasf[zc]
        pre = r + jnp.concatenate([bias] * 4, axis=1)
        sig = jax.nn.sigmoid(pre)
        outc[zc] = pre * sig
        grad = cotf[zc] * sig * (1.0 + pre * (1.0 - sig))
        h, l = split(grad)
        p_hi[zc] = h
        p_lo[zc] = l
        return 0

    lax.fori_loop(0, 4, dense, 0)

    def back_rows(zc):
        both = jnp.concatenate([w_hi[zc], w_lo[zc]], axis=0)
        r = fold(mm(both, p_hi[...].reshape(256, CH), NN))
        return r + mm(w_hi[zc], p_lo[...].reshape(256, CH), NN)

    def send_grad(half, d):
        part = rows_of(half)
        send(gsend.at[d, part], gradf.at[z, part], GRAD[half], at_z(d))

    for d in (2, 1, 3):
        gsend[d] = back_rows(lax.rem(z + d, 4))
        send_grad(0, d)
    for d in (2, 1, 3):
        send_grad(1, d)
    gradf[z] = back_rows(z)

    def out_part():
        return out_h.at[:, pl.ds(pl.multiple_of(z * CH, CH), CH)]

    def weight_rows(zc, _):
        both = jnp.concatenate([s_hi[zc], s_lo[zc]], axis=0)
        r = fold(mm(both, p_hi[...].reshape(256, CH), NT))
        r = r + mm(s_hi[zc], p_lo[...].reshape(256, CH), NT)
        ones = jnp.ones((16, CH), BF16)
        bsum = mm(ones, p_hi[...].reshape(256, CH), NT) + mm(ones, p_lo[...].reshape(256, CH), NT)
        wgs[zc, 0:FL] = r
        wgs[zc, FL:] = bsum[0:8]
        return 0

    lax.fori_loop(0, 4, weight_rows, 0)
    for d in (2, 1, 3):
        send(wgs.at[lax.rem(z + d, 4)], wzr.at[d - 1], WZ, at_z(d))

    for d in (2, 1, 3):
        send(outc.at[lax.rem(z + d, 4)], out_part(), OUT, at_z(d))
    own_out = pltpu.make_async_copy(outc.at[z], out_part(), lsem.at[6])
    own_out.start()


    def take_grad(half):
        arrived(GRAD[half])
        for b in range(NB):
            value = gradf[b // 4, half * H : half * H + H, (b % 4) * B : (b % 4 + 1) * B]
            split_into(x_grad, b, half, value)

    def low_blocks(half):
        tiles(2, LT, 0, half_of(x_grad, half), tile_b, seg)

        def put(g, _):
            for u in range(4):
                bbuf[g * 4 + u, half * H : half * H + H] = block(2, seg, g * 4 + u)
            return 0

        lax.fori_loop(0, 8, put, 0)
        backr[me, half * H : half * H + H] = bbuf[me, half * H : half * H + H]

    take_grad(0)
    low_blocks(0)

    def back_group(half):
        return lambda dx, dy: BACK[half][CHIPS.index((dx, dy)) // 5 if dx + dy > 0 else 2]

    exchange(bbuf, backr, 0, back_group(0))

    take_grad(1)
    low_blocks(1)
    exchange(bbuf, backr, 1, back_group(1))

    tiles(3, HT, LT, lambda s: x_grad[s], tile_b, hseg)

    def hub_blocks(g, _):
        for u in range(4):
            i = g * 4 + u
            hpart[i // 8, lax.rem(i // 2, 4), lax.rem(i, 2)] = block(3, hseg, i)
        return 0

    lax.fori_loop(0, 8, hub_blocks, 0)
    send(hpart.at[:, :, 1 - c], hcore, RED0, at_core)

    arrived(RED0)
    hsum[...] = hpart[:, :, c] + hcore[...]
    for d in (2, 1, 3):
        src = hsum.at[lax.rem(x + d, 4), :, pl.ds(0, 32)]
        send(src, r_a.at[d - 1], RED1, at_x(d))
        src = hsum.at[:, lax.rem(y + d, 4), pl.ds(32, 32)]
        send(src, r_b.at[d - 1], RED1, at_y(d))

    acc[...] = jnp.zeros((FL, VD), F32)

    def add_pair(half, first):
        part = slice(half * H, half * H + H)
        h, l = split(jnp.concatenate([backr[first, part], backr[first + 1, part]], axis=1))
        col = jnp.concatenate([idx_c[first], idx_c[first + 1]], axis=0)
        acc[part, :] += halves(mm(jnp.concatenate([h, l], axis=0), place_t(col), NN))

    def take_back(half, group):
        def step(j, _):
            dx, dy = chip(j)
            add_pair(half, dev(x + 4 - dx, y + 4 - dy, 0))
            return 0

        arrived(BACK[half][group])
        lax.fori_loop(group * 5, group * 5 + 5, step, 0)
        if group == 2:
            add_pair(half, dev(x, y, 0))

    take_back(0, 0)
    arrived(WZ)
    total = wgs[z] + wzr[0] + wzr[1] + wzr[2]
    w1[0] = total[:, :B]
    w1[1] = total[:, B:]
    send(w1.at[1 - c], wcr, WC, at_core)
    take_back(0, 1)
    arrived(WC)
    w2[...] = w1[c] + wcr[...]
    for d in (2, 1, 3):
        send(w2, wxr.at[d - 1], WX, at_x(d))
    take_back(0, 2)

    arrived(RED1)
    t_a[...] = hsum[x, :, 0:32] + r_a[0] + r_a[1] + r_a[2]
    t_b[...] = hsum[:, y, 32:64] + r_b[0] + r_b[1] + r_b[2]
    for d in (2, 1, 3):
        send(t_a.at[lax.rem(y + d, 4)], q_a.at[d - 1], RED2, at_y(d))
        send(t_b.at[lax.rem(x + d, 4)], q_b.at[d - 1], RED2, at_x(d))

    arrived(WX)
    w3[...] = w2[...] + wxr[0] + wxr[1] + wxr[2]
    for d in (2, 1, 3):
        send(w3, wyr.at[d - 1], WY, at_y(d))
    take_back(1, 0)
    take_back(1, 1)
    arrived(WY)
    wfin[c] = w3[...] + wyr[0] + wyr[1] + wyr[2]
    send(wfin.at[c], wfin.at[c], WC2, at_core)
    take_back(1, 2)

    arrived(RED2)
    h_a, l_a = split(t_a[y] + q_a[0] + q_a[1] + q_a[2])
    h_b, l_b = split(t_b[x] + q_b[0] + q_b[1] + q_b[2])
    both = jnp.concatenate([h_a, h_b, l_a, l_b], axis=0)
    acc[...] += fold(mm(both, place_t(hub_c[...]), NN))
    store = pltpu.make_async_copy(acc, fg_h, lsem.at[7])
    store.start()

    arrived(WC2)
    scale = 1.0 / math.sqrt(VD * 32)
    wg_o[:, :B] = wfin[0, 0:FL] * scale
    wg_o[:, B:] = wfin[1, 0:FL] * scale
    row = jnp.concatenate([wfin[0, FL : FL + 1], wfin[1, FL : FL + 1]], axis=1)
    mine = jnp.zeros((1, FL), F32)
    for i in range(4):
        mine = mine + jnp.where(z == i, row[:, i * FL : (i + 1) * FL], 0.0)
    bg_o[...] = mine * scale

    arrived(OUT)
    own_out.wait()
    store.wait()

    for sem in sent:
        remote(size(sem), size(sem), sem, at_core).wait_send()


def hand_over(a, b, c, d, out_a, out_b, out_c, out_d, va, vb, vc, vd, sem_in, sem_out):
    rows = [pl.ds(0, 32), pl.ds(32, 32)]
    trips = [(r.at[h], v.at[h], o.at[h]) for h in rows for r, v, o in [(a, va, out_a), (b, vb, out_b)]]
    trips += [(c, vc, out_c), (d, vd, out_d)]
    fetch = [pltpu.make_async_copy(r, v, sem_in.at[i]) for i, (r, v, _) in enumerate(trips)]
    store = [pltpu.make_async_copy(v, o, sem_out.at[i]) for i, (_, v, o) in enumerate(trips)]
    for copy in fetch:
        copy.start()
    for first, then in zip(fetch, store):
        first.wait()
        then.start()
    for copy in store:
        copy.wait()


def vm(shape, dtype=F32):
    return pltpu.VMEM(shape, dtype)


SCRATCH = [
    vm((32, B), I32), vm((32, B, B), I32), vm((B, B), I32),
    vm((FL, VD)), vm((256, 256)), vm((FL, VD)), vm((LT, B, B)),
    vm((LT + HT, B, 2 * B), BF16), vm((LT + HT, B, 2 * B), BF16),
    vm((32, B), I32), pltpu.SMEM((32, B), I32),
    vm((2 * FL, VD), BF16), vm((32, FL, B)), vm((32, FL, B)),
    vm((4, 4, 2, 32, B)), vm((4, 4, 2, 32, B)), vm((FL, B)),
    vm((32, 2 * FL, B), BF16), vm((32, 2 * FL, B), BF16), vm((LT, H, B)), vm((HT, FL, B)),
    vm((4, FL, CH)), vm((4, FL, CH)), vm((4, FL, CH)), vm((FL, B)), vm((4, FL, B)),
    vm((4, FL, CH), BF16), vm((4, FL, CH), BF16), vm((4, FL, 256), BF16), vm((4, FL, 256), BF16),
    vm((4, FL, 256), BF16), vm((4, FL, 256), BF16), vm((4, FL, CH), BF16), vm((4, FL, CH), BF16),
    vm((4, FL, CH)), vm((4, FL, CH)), vm((4, FL, CH)), vm((NB, 2 * FL, B), BF16),
    vm((32, FL, B)), vm((32, FL, B)), vm((4, 4, 2, FL, B)), vm((4, 4, FL, B)), vm((4, 4, FL, B)),
    vm((3, 4, 32, B)), vm((3, 4, 32, B)), vm((4, 32, B)), vm((4, 32, B)),
    vm((3, 32, B)), vm((3, 32, B)), vm((4, 72, 256)), vm((3, 72, 256)), vm((2, 72, B)),
    vm((72, B)), vm((72, B)), vm((3, 72, B)), vm((72, B)), vm((3, 72, B)), vm((2, 72, B)),
    vm((FL, VD)),
    pltpu.SemaphoreType.DMA((8,)), pltpu.SemaphoreType.DMA((NSEM,)),
    pltpu.SemaphoreType.DMA((NSEM,)),
]


def shards(
    features, weight, bias, cotangent, send_index, send_count, hub_local,
    low_tiles, low_src, low_dst, hub_tiles, hub_src, hub_dst,
):
    hbm = pl.BlockSpec(memory_space=pl.ANY)
    vmem = pl.BlockSpec(memory_space=pltpu.VMEM)
    results = pl.pallas_call(
        kernel,
        out_shape=(
            jax.ShapeDtypeStruct((FL, VD), F32),
            jax.ShapeDtypeStruct((FL, VD), F32),
            jax.ShapeDtypeStruct((FL, 256), F32),
            jax.ShapeDtypeStruct((1, FL), F32),
        ),
        in_specs=[hbm, hbm, vmem, hbm, vmem, vmem, vmem, hbm, hbm, vmem, vmem, vmem, vmem],
        out_specs=(hbm, hbm, vmem, vmem),
        scratch_shapes=SCRATCH,
        compiler_params=pltpu.CompilerParams(
            collective_id=0, has_side_effects=True, vmem_limit_bytes=60 * 2**20
        ),
        cost_estimate=pl.CostEstimate(
            flops=4 * 10**9, bytes_accessed=16 * 2**20, transcendentals=131072
        ),
    )(
        features, weight, bias[None, :], cotangent, send_index.reshape(32, B), send_count,
        hub_local[None, :], low_tiles, hub_tiles,
        low_src[None, :], low_dst[None, :], hub_src[None, :], hub_dst[None, :],
    )
    out, fg, wg, bg = pl.pallas_call(
        hand_over,
        out_shape=tuple(jax.ShapeDtypeStruct(r.shape, r.dtype) for r in results),
        in_specs=[hbm] * 4,
        out_specs=(hbm,) * 4,
        scratch_shapes=[
            vm((FL, VD)), vm((FL, VD)), vm((FL, 256)), vm((1, FL)),
            pltpu.SemaphoreType.DMA((6,)), pltpu.SemaphoreType.DMA((6,)),
        ],
        compiler_params=pltpu.CompilerParams(vmem_limit_bytes=60 * 2**20),
    )(*results)
    return out, fg, wg, bg[0]


def solution(mesh):
    return jax.shard_map(
        shards,
        mesh=mesh,
        in_specs=(
            P("rep", "dom"),
            P(),
            P("rep"),
            P("rep", "dom"),
            P("dom", None),
            P("dom", None),
            P("dom"),
            P("dom", None, None),
            P("dom"),
            P("dom"),
            P("dom", None, None),
            P("dom"),
            P("dom"),
        ),
        out_specs=(P("rep", "dom"), P("rep", "dom"), P("rep", None), P("rep")),
        check_vma=False,
    )
```
